512 devices in a mesh: gx: 8 (over z), gy: 64 (over x, y, core).
Axes of the slice: x: 4, y: 8, z: 8, core: 2. Of those that a mesh axis runs over, the one named last changes fastest.
Arguments:
- features: bfloat16 [1024, 512, 128], P(('gx', 'gy')), may hold values from -6 to 6
- occupancy: int32 [1024, 512], P(('gx', 'gy')), may hold values 0 or 1
- weights: bfloat16 [7, 128, 128], replicated, may hold values from -0.1875 to 0.1875
- cotangent: bfloat16 [1024, 512, 128], P(('gx', 'gy')), may hold values from -6 to 6
- send_count: int32 [512, 64], P(('gx', 'gy')), may hold values from 0 to 1, as said below
- send_face: int32 [512, 64, 1], P(('gx', 'gy')), may hold values from 0 to 11, as said below
- recv_face: int32 [512, 64, 1], P(('gx', 'gy')), may hold values from -1 to 11, as said below
Outputs:
- activated: bfloat16 [1024, 512, 128], P(('gx', 'gy'))
- feature_grad: bfloat16 [1024, 512, 128], P(('gx', 'gy'))
- weight_grad: float32 [7, 128, 128], replicated
The draws below stay inside these ranges and needn't reach their ends.
Inputs may be any that keep to these rules, and one draw needn't show every extreme that they name: `send_count`: at most 1 faces go from one device to one peer, and every device receives 1 faces from some peer. `send_face`: side is the opposite of the side that the receiving slot fills; entries of slots beyond send_count are arbitrary valid faces. `recv_face`: slot s from peer p is used exactly when s < that peer's send_count to this device; the used slots of one device fill distinct ghost faces.
All inputs are finite; a program needn't handle non-finite values. No bound on the sum of `occupancy` on one device may be relied on, other than what follows from the above.
Results may differ from the reference program's by a relative error of at most 0.0049.
Values may be sent and summed in bfloat16 or wider, within the bound.
A program may use at most 64 MiB of HBM per device.

```python
import jax
import jax.numpy as jnp
from jax import lax

CH = 128
NB = 2
CAP = 1
BRICKS = 1024
N_GX = 8
N_GY = 64
DEVICES = 512


def permute_rows(keys, length):

    def permute_one(single_key):
        return jax.random.permutation(single_key, length)
    return jax.vmap(permute_one)(keys)


def halo_plan(key):
    group = N_GY
    devices = N_GX * N_GY
    most = min(6 * NB // CAP, group)
    keys = jax.random.split(key, 5)
    live_peers = jax.random.randint(keys[0], (devices,), most // 2, most + 1)
    orders = permute_rows(jax.random.split(keys[1], devices), group).astype(jnp.int32)
    ranks = jnp.argsort(orders, axis=1, stable=True).astype(jnp.int32)
    counts = jnp.where(ranks < live_peers[:, None], CAP, 0).astype(jnp.int32)
    slot_ids = jnp.arange(CAP, dtype=jnp.int32)
    live = slot_ids[None, None, :] < counts[:, :, None]
    position = jnp.cumsum(live.reshape(devices, group * CAP).astype(jnp.int32), axis=1) - 1
    face_orders = permute_rows(jax.random.split(keys[2], devices), 6 * NB).astype(jnp.int32)
    targets = jnp.take_along_axis(face_orders, jnp.clip(position, 0, 6 * NB - 1), axis=1).reshape(devices, group, CAP)
    received = jnp.where(live, targets, -1).astype(jnp.int32)
    counts_sent = counts.reshape(N_GX, group, group).transpose(0, 2, 1).reshape(devices, group)
    received_sent = received.reshape(N_GX, group, group, CAP).transpose(0, 2, 1, 3).reshape(devices, group, CAP)
    sides = jnp.where(received_sent >= 0, received_sent % 6, jax.random.randint(keys[3], (devices, group, CAP), 0, 6))
    opposite = sides + 1 - 2 * (sides % 2)
    bricks = jax.random.randint(keys[4], (devices, group, CAP), 0, NB)
    sent = (bricks * 6 + opposite).astype(jnp.int32)
    return (counts_sent.astype(jnp.int32), sent, received)


def draw_send_count(key, part):
    return halo_plan(key)[0]


def draw_send_face(key, part):
    return halo_plan(key)[1]


def draw_recv_face(key, part):
    return halo_plan(key)[2]


def plant(array, key, low, high):
    dims = array.shape
    index_at = [jax.random.randint(jax.random.fold_in(key, axis), (), 0, dims[axis]) for axis in range(len(dims))]
    array = array.at[tuple(index_at)].set(low)
    longest = dims.index(max(dims))
    index_at[longest] = (index_at[longest] + 1) % dims[longest]
    return array.at[tuple(index_at)].set(high)


def levels(own_key, shape, cuts, low, largest):
    def one(axis_at, shards_of):
        heights = jax.random.uniform(jax.random.fold_in(jax.random.fold_in(own_key, 6), axis_at), (shards_of,), jnp.float32, low / len(cuts), largest / len(cuts))
        return jnp.repeat(jnp.exp(heights), shape[axis_at] // shards_of).reshape((-1,) + (1,) * (len(shape) - axis_at - 1))

    factor_of = one(*cuts[0])
    for cut in cuts[1:]:
        factor_of = factor_of * one(*cut)
    return factor_of


def noise(key, dims, deviation, limit, cuts=(), kind=jnp.bfloat16):
    values = jax.random.normal(key, dims, jnp.float32) * deviation
    if len(cuts) > 0:
        values = levels(key, dims, cuts, -0.22, 0.18) * values
    return jnp.clip(values, min=-limit, max=limit).astype(kind)


def setup_inputs(seed: int = 0) -> dict:
    arg_keys = jax.random.split(jax.random.key(seed), 8)
    return {
        "features": noise(arg_keys[0], (BRICKS, 512, CH), 1.0, 6.0, ((0, 512),)),
        "occupancy": plant((jax.random.randint(arg_keys[1], (BRICKS, 512), 0, 4) < 3).astype(jnp.int32), jax.random.fold_in(arg_keys[1], 1), 0, 1),
        "weights": noise(arg_keys[2], (7, CH, CH), (7 * CH) ** -0.5, 0.1875),
        "cotangent": noise(arg_keys[3], (BRICKS, 512, CH), 1.0, 6.0, ((0, 512),)),
        "send_count": draw_send_count(jax.random.fold_in(arg_keys[7], 71), 0),
        "send_face": draw_send_face(jax.random.fold_in(arg_keys[7], 71), 0),
        "recv_face": draw_recv_face(jax.random.fold_in(arg_keys[7], 71), 0),
    }


tap_starts = ((1, 1, 1), (0, 1, 1), (2, 1, 1), (1, 0, 1), (1, 2, 1), (1, 1, 0), (1, 1, 2))


def side_faces(cube):
    bricks = cube.shape[0]
    width = cube.shape[-1]
    planes = [cube[:, 0], cube[:, 7], cube[:, :, 0], cube[:, :, 7], cube[:, :, :, 0], cube[:, :, :, 7]]
    return jnp.stack([plane.reshape(bricks, 64 * width) for plane in planes], axis=1)


def padded_cube(cube, ghost):
    bricks = cube.shape[0]
    width = cube.shape[-1]
    planes = ghost.reshape(bricks, 6, 8, 8, width)
    padded = jnp.pad(cube, ((0, 0), (1, 1), (1, 1), (1, 1), (0, 0)))
    padded = padded.at[:, 0, 1:9, 1:9].set(planes[:, 0])
    padded = padded.at[:, 9, 1:9, 1:9].set(planes[:, 1])
    padded = padded.at[:, 1:9, 0, 1:9].set(planes[:, 2])
    padded = padded.at[:, 1:9, 9, 1:9].set(planes[:, 3])
    padded = padded.at[:, 1:9, 1:9, 0].set(planes[:, 4])
    padded = padded.at[:, 1:9, 1:9, 9].set(planes[:, 5])
    return padded


def tap_views(padded):
    return [padded[:, sx:sx + 8, sy:sy + 8, sz:sz + 8] for sx, sy, sz in tap_starts]


def convolve(views, weights):
    width = weights.shape[-1]
    total = jnp.zeros((views[0].size // width, width), jnp.float32)
    for tap_index in range(7):
        total = total + jnp.dot(views[tap_index].reshape(-1, width), weights[tap_index], preferred_element_type=jnp.float32)
    return total.reshape(views[0].shape)


def add_layers(cube, planes):
    cube = cube.at[:, 0].add(planes[:, 0])
    cube = cube.at[:, 7].add(planes[:, 1])
    cube = cube.at[:, :, 0].add(planes[:, 2])
    cube = cube.at[:, :, 7].add(planes[:, 3])
    cube = cube.at[:, :, :, 0].add(planes[:, 4])
    cube = cube.at[:, :, :, 7].add(planes[:, 5])
    return cube


def place_ghosts(received, recv_rows, face_total):
    group, slots, flat = received.shape
    flat_rows = recv_rows.reshape(-1)
    target = jnp.where(flat_rows >= 0, flat_rows, face_total).astype(jnp.int32)
    source_slot = jnp.full((face_total + 1,), group * slots, jnp.int32).at[target].set(jnp.arange(group * slots, dtype=jnp.int32))
    stacked = jnp.concatenate([received.reshape(group * slots, flat), jnp.zeros((1, flat), received.dtype)], axis=0)
    return stacked[source_slot[:face_total]]


def transpose_conv(delta, weights):
    bricks = delta.shape[0]
    width = weights.shape[-1]
    flat_delta = delta.reshape(-1, width)
    grad_pad = jnp.zeros((bricks, 10, 10, 10, width), jnp.float32)
    for tap_index in range(7):
        sx, sy, sz = tap_starts[tap_index]
        product = lax.dot_general(flat_delta, weights[tap_index], (((1,), (1,)), ((), ())), preferred_element_type=jnp.float32)
        grad_pad = grad_pad.at[:, sx:sx + 8, sy:sy + 8, sz:sz + 8].add(product.reshape(delta.shape))
    return grad_pad[:, 1:9, 1:9, 1:9]


def face_gradients(back, send_rows, send_counts, weights, face_total):
    group, slots, flat = back.shape
    width = weights.shape[-1]
    valid = jnp.arange(slots, dtype=jnp.int32)[None, :] < send_counts[:, None]
    sides = send_rows % 6
    taps = 1 + sides + 1 - 2 * (sides % 2)
    chosen = weights[taps.reshape(-1)]
    contrib = jnp.einsum("sfd,scd->sfc", back.reshape(group * slots, 64, width), chosen, preferred_element_type=jnp.float32)
    contrib = jnp.where(valid.reshape(-1, 1, 1), contrib, jnp.zeros_like(contrib))
    target = jnp.where(valid, send_rows, face_total).reshape(-1).astype(jnp.int32)
    summed = jnp.zeros((face_total + 1, 64, width), jnp.float32).at[target].add(contrib)
    return summed[:face_total]


def local_forward(cube, ghost, weights, mask_cube, cot_cube):
    views = tap_views(padded_cube(cube, ghost))
    preact = convolve(views, weights)
    sigma = jax.nn.sigmoid(preact)
    activated = (mask_cube * preact * sigma).astype(jnp.bfloat16)
    delta = (cot_cube.astype(jnp.float32) * mask_cube * sigma * (1.0 + preact * (1.0 - sigma))).astype(jnp.bfloat16)
    return views, activated, delta


def reference(features, occupancy, weights, cotangent, send_count, send_face, recv_face):
    width = CH
    group = N_GY
    face_total = NB * 6
    occupied = (occupancy > 0)[..., None]
    masked = jnp.where(occupied, features, jnp.zeros_like(features))
    cubes = masked.reshape(DEVICES, NB, 8, 8, 8, width)
    masks = occupied.astype(jnp.float32).reshape(DEVICES, NB, 8, 8, 8, 1)
    cots = cotangent.reshape(DEVICES, NB, 8, 8, 8, width)
    members = jnp.arange(group, dtype=jnp.int32)
    slot_ids = jnp.arange(CAP, dtype=jnp.int32)

    def ghost_for(device):
        outer = device // group
        inner = device % group
        sources = outer * group + members
        chosen = send_face[sources, inner]
        counts = send_count[sources, inner]
        faces = side_faces(cubes[sources].reshape(group * NB, 8, 8, 8, width)).reshape(group, face_total, 64 * width)
        picked = jnp.take_along_axis(faces, chosen[:, :, None], axis=1)
        valid = slot_ids[None, :] < counts[:, None]
        picked = jnp.where(valid[..., None], picked, jnp.zeros_like(picked))
        return place_ghosts(picked, recv_face[device], face_total).reshape(NB, 6, 64 * width)

    def first_pass(device):
        ghost = ghost_for(device)
        views, activated, delta = local_forward(cubes[device], ghost, weights, masks[device], cots[device])
        return activated, side_faces(delta).reshape(face_total, 64 * width)

    activated_all, delta_faces = lax.map(first_pass, jnp.arange(DEVICES, dtype=jnp.int32))

    def second_pass(device):
        ghost = ghost_for(device)
        views, activated, delta = local_forward(cubes[device], ghost, weights, masks[device], cots[device])
        flat_delta = delta.reshape(-1, width)
        partial_grad = jnp.stack([lax.dot_general(view.reshape(-1, width), flat_delta, (((0,), (0,)), ((), ())), preferred_element_type=jnp.float32) for view in views])
        inner_grad = transpose_conv(delta, weights)
        outer = device // group
        inner = device % group
        receivers = outer * group + members
        their_rows = recv_face[receivers, inner]
        fetched = delta_faces[receivers[:, None], jnp.maximum(their_rows, 0)]
        back = jnp.where((their_rows >= 0)[..., None], fetched, jnp.zeros_like(fetched))
        extra = face_gradients(back, send_face[device], send_count[device], weights, face_total).reshape(NB, 6, 8, 8, width)
        total_grad = add_layers(inner_grad, extra)
        feature_grad = (masks[device] * total_grad).astype(jnp.bfloat16)
        return feature_grad, partial_grad

    grads_all, partials = lax.map(second_pass, jnp.arange(DEVICES, dtype=jnp.int32))
    scale = float(BRICKS * 512) ** -0.5
    weight_grad = jnp.sum(partials, axis=0) * scale
    return activated_all.reshape(BRICKS, 512, width), grads_all.reshape(BRICKS, 512, width), weight_grad
```

```python
import functools

import jax
import jax.numpy as jnp
from jax import lax
from jax.experimental import pallas as pl
from jax.experimental.pallas import tpu as pltpu
from jax.sharding import PartitionSpec as P

XN = 4
YN = 8
CN = 2
MESH = pl.DeviceIdType.MESH
CH = 128
NB = 2
FACES = NB * 6
VOX = 512
ROWS = NB * VOX
TAPS = 7
OPPOSITE = (0, 2, 1, 4, 3, 6, 5)
BF = jnp.bfloat16
F32 = jnp.float32


def product(a, b):
    return jnp.dot(a, b, preferred_element_type=F32)


def cut_faces(cube, faces):
    for b in range(NB):
        base = b * VOX
        body = cube[base : base + VOX, :].reshape(8, 8, 8, CH)
        faces[b * 6 + 0] = cube[base : base + 64, :].astype(BF)
        faces[b * 6 + 1] = cube[base + 448 : base + 512, :].astype(BF)
        faces[b * 6 + 2] = body[:, 0].reshape(64, CH).astype(BF)
        faces[b * 6 + 3] = body[:, 7].reshape(64, CH).astype(BF)
        faces[b * 6 + 4] = cube[pl.ds(base, 64, stride=8), :].astype(BF)
        faces[b * 6 + 5] = cube[pl.ds(base + 7, 64, stride=8), :].astype(BF)


def build_views(cube, ghost, shifted, views):
    for b in range(NB):
        base = b * VOX
        rows = slice(base, base + VOX)
        g = b * 6
        body = cube[rows, :]
        solid = body.reshape(8, 8, 8, CH)
        views[rows, 0:128] = body.astype(BF)
        views[base : base + 64, 128:256] = ghost[g + 0].astype(BF)
        views[base + 64 : base + 512, 128:256] = cube[base : base + 448, :].astype(BF)
        views[base : base + 448, 256:384] = cube[base + 64 : base + 512, :].astype(BF)
        views[base + 448 : base + 512, 256:384] = ghost[g + 1].astype(BF)
        low = ghost[g + 2].reshape(8, 1, 8, CH)
        high = ghost[g + 3].reshape(8, 1, 8, CH)
        views[rows, 384:512] = jnp.concatenate([low, solid[:, :7]], axis=1).reshape(VOX, CH).astype(BF)
        views[rows, 512:640] = jnp.concatenate([solid[:, 1:], high], axis=1).reshape(VOX, CH).astype(BF)
        shifted[1:VOX, :] = cube[base : base + VOX - 1, :]
        shifted[pl.ds(0, 64, stride=8), :] = ghost[g + 4]
        views[rows, 640:768] = shifted[...].astype(BF)
        shifted[0 : VOX - 1, :] = cube[base + 1 : base + VOX, :]
        shifted[pl.ds(7, 64, stride=8), :] = ghost[g + 5]
        views[rows, 768:896] = shifted[...].astype(BF)


def kernel(
    zn, gn, scale,
    feat, occ, wcat, cot, count, sface, rface,
    act_out, grad_out, wg_out,
    mask, cube, faces, out1, out2, in1, in2, ghost, shifted, views, wback, delta_t, run, prev,
    part, zsend, zrecv, xsend, xrecv, yrecv, xgath, zgath,
    sems,
):
    z = lax.axis_index("gx")
    me = lax.axis_index("gy")
    xc_n = XN * CN
    my_x = me // (YN * CN)
    my_y = lax.rem(me // CN, YN)
    my_c = lax.rem(me, CN)
    my_xc = my_x * CN + my_c
    share = TAPS * CH // zn
    piece = xsend.shape[1]

    def z_peer(k):
        return lax.rem(z + k, zn)

    def xc_peer(k):
        return lax.rem(my_xc + k, xc_n)

    def xc_device(xc):
        return (xc // CN * YN + my_y) * CN + lax.rem(xc, CN)

    def y_peer(k):
        return lax.rem(my_y + k, YN)

    def y_device(y):
        return (my_x * YN + y) * CN + my_c

    barrier = pltpu.get_barrier_semaphore()

    def greet_group(k, _):
        pl.semaphore_signal(barrier, inc=1, device_id=(z, lax.rem(me + k, gn)), device_id_type=MESH)
        return 0

    def greet_z(k, _):
        pl.semaphore_signal(barrier, inc=1, device_id=(z_peer(k), me), device_id_type=MESH)
        return 0

    lax.fori_loop(1, gn, greet_group, 0)
    lax.fori_loop(1, zn, greet_z, 0)

    diagonal = lax.broadcasted_iota(jnp.int32, (CH, CH), 0) == lax.broadcasted_iota(jnp.int32, (CH, CH), 1)
    ones = jnp.ones((CH, CH), BF)
    for b in range(NB):
        for i in range(VOX // CH):
            row = (occ[b : b + 1, i * CH : (i + 1) * CH] > 0).astype(F32)
            spread = jnp.where(diagonal, jnp.broadcast_to(row, (CH, CH)), 0.0).astype(BF)
            at = b * VOX + i * CH
            flags = product(spread, ones)
            mask[at : at + CH, :] = flags
            cube[at : at + CH, :] = jnp.where(flags > 0, feat[at : at + CH, :].astype(F32), 0.0)
    cut_faces(cube, faces)

    def fill_sent(q, _):
        out1[q] = faces[sface[q]]
        return 0

    lax.fori_loop(0, gn, fill_sent, 0)
    pl.semaphore_wait(barrier, gn - 1 + zn - 1)

    def exchange(out, landed, send_sem, recv_sem):
        def one(k, _):
            q = lax.rem(me + k, gn)
            pltpu.make_async_remote_copy(
                src_ref=out.at[q], dst_ref=landed.at[me], send_sem=send_sem, recv_sem=recv_sem,
                device_id=(z, q), device_id_type=MESH,
            ).start()
            return 0

        lax.fori_loop(1, gn, one, 0)

    def wait_for(ref, sem):
        pltpu.make_async_copy(ref, ref, sem).wait()

    exchange(out1, in1, sems.at[0], sems.at[1])
    in1[me] = out1[me]

    for t in range(TAPS):
        o = OPPOSITE[t]
        wback[t * CH : (t + 1) * CH, :] = wcat[o * CH : (o + 1) * CH, :].astype(F32).T.astype(BF)

    def find_source(p, found):
        row = rface[p]
        return tuple(jnp.where(row == f, p, found[f]) for f in range(FACES))

    source = lax.fori_loop(0, gn, find_source, tuple(jnp.int32(-1) for _ in range(FACES)))

    def chain(q, last):
        face = jnp.where(count[q] > 0, sface[q], FACES)
        before = jnp.int32(0)
        for f in range(FACES):
            before = jnp.where(face == f, last[f], before)
        prev[q] = before
        return tuple(jnp.where(face == f, q + 1, last[f]) for f in range(FACES))

    last = lax.fori_loop(0, gn, chain, tuple(jnp.int32(0) for _ in range(FACES)))

    wait_for(in1.at[pl.ds(0, gn - 1)], sems.at[1])
    for f in range(FACES):
        taken = in1[jnp.maximum(source[f], 0)].astype(F32)
        ghost[f] = jnp.where(source[f] >= 0, taken, 0.0)

    build_views(cube, ghost, shifted, views)
    for b in range(2 * NB):
        rows = slice(b * VOX // 2, (b + 1) * VOX // 2)
        preact = product(views[rows, :], wcat[...])
        sigma = jax.nn.sigmoid(preact)
        flags = mask[rows, :]
        act_out[rows, :] = (flags * preact * sigma).astype(BF)
        delta = (cot[rows, :].astype(F32) * flags * sigma * (1.0 + preact * (1.0 - sigma))).astype(BF)
        cube[rows, :] = delta.astype(F32)
    cut_faces(cube, faces)

    def fill_returned(p, _):
        out2[p] = faces[jnp.maximum(rface[p], 0)]
        return 0

    lax.fori_loop(0, gn, fill_returned, 0)
    exchange(out2, in2, sems.at[2], sems.at[3])
    in2[me] = out2[me]

    delta_t[...] = cube[...].T.astype(BF)
    for t in range(TAPS):
        part[t * CH : (t + 1) * CH, :] = product(delta_t[...], views[:, t * CH : (t + 1) * CH]).T
    zsend[...] = part[...].astype(BF).reshape(zn, share, CH)

    def send_z(out, at_out, landed, send_sem, recv_sem):
        def one(k, _):
            q = z_peer(k)
            pltpu.make_async_remote_copy(
                src_ref=out.at[q] if at_out else out.at[z], dst_ref=landed.at[z], send_sem=send_sem, recv_sem=recv_sem,
                device_id=(q, me), device_id_type=MESH,
            ).start()
            return 0

        lax.fori_loop(1, zn, one, 0)

    def send_xc(out, at_out, landed, send_sem, recv_sem):
        def one(k, _):
            q = xc_peer(k)
            pltpu.make_async_remote_copy(
                src_ref=out.at[q] if at_out else out.at[my_xc], dst_ref=landed.at[my_xc], send_sem=send_sem,
                recv_sem=recv_sem, device_id=(z, xc_device(q)), device_id_type=MESH,
            ).start()
            return 0

        lax.fori_loop(1, xc_n, one, 0)

    send_z(zsend, True, zrecv, sems.at[4], sems.at[5])
    zrecv[z] = jnp.zeros((share, CH), BF)
    own = part[pl.ds(pl.multiple_of(z * share, 16), share), :]
    wait_for(zrecv.at[pl.ds(0, zn - 1)], sems.at[5])
    total = own
    for k in range(zn):
        total = total + zrecv[k].astype(F32)
    padding = jnp.zeros((piece * xc_n - share, CH), F32)
    xsend[...] = jnp.concatenate([total, padding], axis=0).reshape(xc_n, piece, CH)
    send_xc(xsend, True, xrecv, sems.at[6], sems.at[7])
    xrecv[my_xc] = xsend[my_xc]
    wait_for(xrecv.at[pl.ds(0, xc_n - 1)], sems.at[7])
    total = xrecv[0]
    for k in range(1, xc_n):
        total = total + xrecv[k]
    yrecv[my_y] = total

    def send_y(k, _):
        pltpu.make_async_remote_copy(
            src_ref=yrecv.at[my_y], dst_ref=yrecv.at[my_y], send_sem=sems.at[8], recv_sem=sems.at[9],
            device_id=(z, y_device(y_peer(k))), device_id_type=MESH,
        ).start()
        return 0

    lax.fori_loop(1, YN, send_y, 0)
    wait_for(yrecv.at[pl.ds(0, YN - 1)], sems.at[9])
    total = yrecv[0]
    for k in range(1, YN):
        total = total + yrecv[k]
    xgath[my_xc] = total.astype(BF)
    send_xc(xgath, False, xgath, sems.at[10], sems.at[11])
    wait_for(xgath.at[pl.ds(0, xc_n - 1)], sems.at[11])
    zgath[z] = xgath[...].reshape(xc_n * piece, CH)[:share]
    send_z(zgath, False, zgath, sems.at[12], sems.at[13])
    wait_for(zgath.at[pl.ds(0, zn - 1)], sems.at[13])
    wg_out[...] = zgath[...].reshape(TAPS * CH, CH).astype(F32) * scale

    wait_for(in2.at[pl.ds(0, gn - 1)], sems.at[3])
    run[0] = jnp.zeros((64, CH), F32)

    def add_up(q, _):
        run[q + 1] = run[prev[q]] + in2[q].astype(F32)
        return 0

    lax.fori_loop(0, gn, add_up, 0)
    for f in range(FACES):
        ghost[f] = run[last[f]]
    build_views(cube, ghost, shifted, views)
    for b in range(2 * NB):
        rows = slice(b * VOX // 2, (b + 1) * VOX // 2)
        grad = product(views[rows, :], wback[...])
        grad_out[rows, :] = (mask[rows, :] * grad).astype(BF)

    wait_for(out1.at[pl.ds(0, gn - 1)], sems.at[0])
    wait_for(out2.at[pl.ds(0, gn - 1)], sems.at[2])
    wait_for(zsend.at[pl.ds(0, zn - 1)], sems.at[4])
    wait_for(xsend.at[pl.ds(0, xc_n - 1)], sems.at[6])
    wait_for(yrecv.at[pl.ds(0, YN - 1)], sems.at[8])
    wait_for(xgath.at[pl.ds(0, xc_n - 1)], sems.at[10])
    wait_for(zgath.at[pl.ds(0, zn - 1)], sems.at[12])


def on_device(zn, gn, features, occupancy, weights, cotangent, send_count, send_face, recv_face):
    vmem = pl.BlockSpec(memory_space=pltpu.VMEM)
    smem = pl.BlockSpec(memory_space=pltpu.SMEM)
    xc_n = XN * CN
    share = TAPS * CH // zn
    piece = -(-share // (16 * xc_n)) * 16
    scale = float(zn * gn * ROWS) ** (-0.5)
    activated, grad, weight_grad = pl.pallas_call(
        functools.partial(kernel, zn, gn, scale),
        out_shape=(
            jax.ShapeDtypeStruct((ROWS, CH), BF),
            jax.ShapeDtypeStruct((ROWS, CH), BF),
            jax.ShapeDtypeStruct((TAPS * CH, CH), F32),
        ),
        in_specs=[vmem, vmem, vmem, vmem, smem, smem, smem],
        out_specs=(vmem, vmem, vmem),
        scratch_shapes=[
            pltpu.VMEM((ROWS, CH), F32),
            pltpu.VMEM((ROWS, CH), F32),
            pltpu.VMEM((FACES, 64, CH), BF),
            pltpu.VMEM((gn, 64, CH), BF),
            pltpu.VMEM((gn, 64, CH), BF),
            pltpu.VMEM((gn, 64, CH), BF),
            pltpu.VMEM((gn, 64, CH), BF),
            pltpu.VMEM((FACES, 64, CH), F32),
            pltpu.VMEM((VOX, CH), F32),
            pltpu.VMEM((ROWS, TAPS * CH), BF),
            pltpu.VMEM((TAPS * CH, CH), BF),
            pltpu.VMEM((CH, ROWS), BF),
            pltpu.VMEM((gn + 1, 64, CH), F32),
            pltpu.SMEM((gn,), jnp.int32),
            pltpu.VMEM((TAPS * CH, CH), F32),
            pltpu.VMEM((zn, share, CH), BF),
            pltpu.VMEM((zn, share, CH), BF),
            pltpu.VMEM((xc_n, piece, CH), F32),
            pltpu.VMEM((xc_n, piece, CH), F32),
            pltpu.VMEM((YN, piece, CH), F32),
            pltpu.VMEM((xc_n, piece, CH), BF),
            pltpu.VMEM((zn, share, CH), BF),
            pltpu.SemaphoreType.DMA((14,)),
        ],
        compiler_params=pltpu.CompilerParams(
            collective_id=0, has_side_effects=True, vmem_limit_bytes=40 * 1024 * 1024
        ),
        cost_estimate=pl.CostEstimate(
            flops=6 * ROWS * TAPS * CH * CH, bytes_accessed=2000000, transcendentals=ROWS * CH
        ),
    )(
        features.reshape(ROWS, CH),
        occupancy,
        weights.reshape(TAPS * CH, CH),
        cotangent.reshape(ROWS, CH),
        send_count.reshape(gn),
        send_face.reshape(gn),
        recv_face.reshape(gn),
    )
    return (
        activated.reshape(NB, VOX, CH),
        grad.reshape(NB, VOX, CH),
        weight_grad.reshape(TAPS, CH, CH),
    )


def solution(mesh):
    zn, gn = mesh.shape["gx"], mesh.shape["gy"]
    split = P(("gx", "gy"), None, None)
    return jax.shard_map(
        functools.partial(on_device, zn, gn),
        mesh=mesh,
        in_specs=(split, P(("gx", "gy"), None), P(), split, P(("gx", "gy"), None), split, split),
        out_specs=(split, split, P()),
        check_vma=False,
    )
```

```python
import functools

import jax
import jax.numpy as jnp
from jax import lax
from jax.experimental import pallas as pl
from jax.experimental.pallas import tpu as pltpu
from jax.sharding import PartitionSpec as P

XN = 4
YN = 8
CN = 2
MESH = pl.DeviceIdType.MESH
CH = 128
NB = 2
FACES = NB * 6
VOX = 512
ROWS = NB * VOX
TAPS = 7
OPPOSITE = (0, 2, 1, 4, 3, 6, 5)
BF = jnp.bfloat16
F32 = jnp.float32


def product(a, b):
    return jnp.dot(a, b, preferred_element_type=F32)


def cut_faces(cube, faces):
    for b in range(NB):
        base = b * VOX
        body = cube[base : base + VOX, :].reshape(8, 8, 8, CH)
        faces[b * 6 + 0] = cube[base : base + 64, :].astype(BF)
        faces[b * 6 + 1] = cube[base + 448 : base + 512, :].astype(BF)
        faces[b * 6 + 2] = body[:, 0].reshape(64, CH).astype(BF)
        faces[b * 6 + 3] = body[:, 7].reshape(64, CH).astype(BF)
        faces[b * 6 + 4] = cube[pl.ds(base, 64, stride=8), :].astype(BF)
        faces[b * 6 + 5] = cube[pl.ds(base + 7, 64, stride=8), :].astype(BF)


def build_views(cube, ghost, shifted, views):
    for b in range(NB):
        base = b * VOX
        rows = slice(base, base + VOX)
        g = b * 6
        body = cube[rows, :]
        solid = body.reshape(8, 8, 8, CH)
        views[rows, 0:128] = body.astype(BF)
        views[base : base + 64, 128:256] = ghost[g + 0].astype(BF)
        views[base + 64 : base + 512, 128:256] = cube[base : base + 448, :].astype(BF)
        views[base : base + 448, 256:384] = cube[base + 64 : base + 512, :].astype(BF)
        views[base + 448 : base + 512, 256:384] = ghost[g + 1].astype(BF)
        low = ghost[g + 2].reshape(8, 1, 8, CH)
        high = ghost[g + 3].reshape(8, 1, 8, CH)
        views[rows, 384:512] = jnp.concatenate([low, solid[:, :7]], axis=1).reshape(VOX, CH).astype(BF)
        views[rows, 512:640] = jnp.concatenate([solid[:, 1:], high], axis=1).reshape(VOX, CH).astype(BF)
        shifted[1:VOX, :] = cube[base : base + VOX - 1, :]
        shifted[pl.ds(0, 64, stride=8), :] = ghost[g + 4]
        views[rows, 640:768] = shifted[...].astype(BF)
        shifted[0 : VOX - 1, :] = cube[base + 1 : base + VOX, :]
        shifted[pl.ds(7, 64, stride=8), :] = ghost[g + 5]
        views[rows, 768:896] = shifted[...].astype(BF)


ROW_OF = (0, 4, -1, 1, -2, 2, -3, 3)
PIECES = 3


def kernel(
    zn, gn, scale,
    feat_in, occ_in, wcat_in, cot_in, count_in, sface_in, rface_in,
    act_out, grad_out, wg_out,
    feat, occ, wcat, cot, count, sface, rface,
    mask, cube, ghost, shifted, views, wback, delta_t, run, prev, slot_face, slot_row, meta_out, meta_in,
    faces_a, faces_b, rows_a, rows_b, got_a, got_b, up_a, down_a, up_b, down_b,
    csend, crecv, zsend, zrecv, xgot, ygot, zgath, cgath,
    load_sems, chain_a, chain_b, sems,
):
    z = lax.axis_index("gx")
    me = lax.axis_index("gy")
    xc_n = XN * CN
    my_x = me // (YN * CN)
    my_y = lax.rem(me // CN, YN)
    my_c = lax.rem(me, CN)
    my_xc = my_x * CN + my_c
    half = TAPS * CH // CN
    share = half // zn

    def wrap_y(offset):
        return lax.rem(my_y + offset + YN, YN)

    def at(xc, y):
        return (xc // CN * YN + y) * CN + lax.rem(xc, CN)

    def xc_peer(k):
        return lax.rem(my_xc + k, xc_n)

    def z_peer(k):
        return lax.rem(z + k, zn)

    def repeat(low, high, body):
        def step(i, _):
            body(i)
            return 0

        lax.fori_loop(low, high, step, 0)

    def send(src, dst, send_sem, recv_sem, to):
        copy = pltpu.make_async_remote_copy(
            src_ref=src, dst_ref=dst, send_sem=send_sem, recv_sem=recv_sem, device_id=to, device_id_type=MESH
        )
        copy.start()

    def wait_for(ref, sem):
        pltpu.make_async_copy(ref, ref, sem).wait()

    barrier = pltpu.get_barrier_semaphore()

    def greet(to):
        pl.semaphore_signal(barrier, inc=1, device_id=to, device_id_type=MESH)

    repeat(1, YN, lambda k: greet((z, at(my_xc, wrap_y(k)))))
    repeat(1, xc_n, lambda k: greet((z, at(xc_peer(k), my_y))))
    repeat(1, xc_n, lambda k: greet((z, at(xc_peer(k), wrap_y(4)))))
    if zn > 1:
        repeat(1, zn, lambda k: greet((z_peer(k), me)))

    loads = [
        pltpu.make_async_copy(src, dst, load_sems.at[i])
        for i, (src, dst) in enumerate(
            [(occ_in, occ), (feat_in, feat), (sface_in, sface), (rface_in, rface), (count_in, count), (wcat_in, wcat),
             (cot_in, cot)]
        )
    ]
    for load in loads:
        load.start()

    diagonal = lax.broadcasted_iota(jnp.int32, (CH, CH), 0) == lax.broadcasted_iota(jnp.int32, (CH, CH), 1)
    ones = jnp.ones((CH, CH), BF)
    loads[0].wait()
    loads[1].wait()
    for b in range(NB):
        for i in range(VOX // CH):
            row = (occ[b : b + 1, i * CH : (i + 1) * CH] > 0).astype(F32)
            spread = jnp.where(diagonal, jnp.broadcast_to(row, (CH, CH)), 0.0).astype(BF)
            place = b * VOX + i * CH
            flags = product(spread, ones)
            mask[place : place + CH, :] = flags
            cube[place : place + CH, :] = jnp.where(flags > 0, feat[place : place + CH, :].astype(F32), 0.0)
    cut_faces(cube, faces_a)
    loads[2].wait()
    loads[3].wait()
    loads[4].wait()

    def fill_meta(y):
        for xc in range(xc_n):
            meta_out[y, xc] = sface[at(jnp.int32(xc), y)]
            meta_out[y, xc_n + xc] = jnp.maximum(rface[at(jnp.int32(xc), y)], 0)

    repeat(0, YN, fill_meta)

    def start_exchange(faces, column, rows, got, up, down, chain, row_sems):
        for p in range(PIECES):
            part = pl.ds(p * 4, 4)
            send(faces.at[part], up[0].at[part], chain.at[0], chain.at[6 + p], (z, at(my_xc, wrap_y(1))))
            send(faces.at[part], down[0].at[part], chain.at[3], chain.at[6 + 9 + p], (z, at(my_xc, wrap_y(-1))))
        far = wrap_y(4)

        def pick(xc):
            rows[xc, 0] = faces[meta_out[my_y, column + xc]]
            rows[xc, 1] = faces[meta_out[far, column + xc]]

        repeat(0, xc_n, pick)

        def ship(k):
            xc = xc_peer(k)
            send(rows.at[xc, 1], got.at[my_xc, 1], row_sems.at[0], row_sems.at[1], (z, at(xc, far)))

        repeat(0, xc_n, ship)

        def ship_own(k):
            xc = xc_peer(k)
            send(rows.at[xc, 0], got.at[my_xc, 0], row_sems.at[0], row_sems.at[1], (z, at(xc, my_y)))

        repeat(1, xc_n, ship_own)
        got[my_xc, 0] = rows[my_xc, 0]

    def step_exchange(d, column, rows, got, up, down, chain, row_sems):
        for p in range(PIECES):
            part = pl.ds(p * 4, 4)
            wait_for(up[d - 1].at[part], chain.at[6 + (d - 1) * 3 + p])
            if d < 3:
                send(up[d - 1].at[part], up[d].at[part], chain.at[d], chain.at[6 + d * 3 + p],
                     (z, at(my_xc, wrap_y(1))))
            wait_for(down[d - 1].at[part], chain.at[6 + 9 + (d - 1) * 3 + p])
            if d < 3:
                send(down[d - 1].at[part], down[d].at[part], chain.at[3 + d], chain.at[6 + 9 + d * 3 + p],
                     (z, at(my_xc, wrap_y(-1))))
        low, high = wrap_y(-d), wrap_y(d)

        def pick(xc):
            rows[xc, 2 * d] = up[d - 1][meta_in[low, column + xc]]
            rows[xc, 2 * d + 1] = down[d - 1][meta_in[high, column + xc]]

        repeat(0, xc_n, pick)
        pair = pl.ds(2 * d, 2)

        def ship(k):
            xc = xc_peer(k)
            send(rows.at[xc, pair], got.at[my_xc, pair], row_sems.at[0], row_sems.at[1], (z, at(xc, my_y)))

        repeat(1, xc_n, ship)
        got[my_xc, pair] = rows[my_xc, pair]

    remote_faces = (xc_n - 1) * 7 + xc_n

    def flat(ref):
        return ref.reshape(xc_n * 8, 64, CH).at[pl.ds(0, remote_faces)]

    def drain(rows, up, down, chain, row_sems):
        for d in range(3):
            wait_for(up[d], chain.at[d])
            wait_for(down[d], chain.at[3 + d])
        wait_for(flat(rows), row_sems.at[0])

    pl.semaphore_wait(barrier, (YN - 1) + 2 * (xc_n - 1) + (zn - 1))
    sems_a, sems_b = sems.at[pl.ds(0, 2)], sems.at[pl.ds(2, 2)]
    for d in (1, -1, 2, -2, 3, -3):
        y = wrap_y(d)
        send(meta_out.at[y], meta_in.at[my_y], sems.at[4], sems.at[5], (z, at(my_xc, y)))
    first = (rows_a, got_a, up_a, down_a, chain_a, sems_a)
    second = (rows_b, got_b, up_b, down_b, chain_b, sems_b)
    start_exchange(faces_a, 0, *first)

    def list_slots(xc):
        for s in range(8):
            p = at(xc, wrap_y(ROW_OF[s]))
            slot_row[xc * 8 + s] = rface[p]
            slot_face[xc * 8 + s] = jnp.where(count[p] > 0, sface[p], FACES)

    repeat(0, xc_n, list_slots)

    def find_source(j, found):
        row = slot_row[j]
        return tuple(jnp.where(row == f, j, found[f]) for f in range(FACES))

    source = lax.fori_loop(0, gn, find_source, tuple(jnp.int32(-1) for _ in range(FACES)))
    loads[5].wait()
    loads[6].wait()
    wait_for(meta_in.at[pl.ds(0, 6)], sems.at[5])
    step_exchange(1, 0, *first)
    for t in range(TAPS):
        o = OPPOSITE[t]
        wback[t * CH : (t + 1) * CH, :] = wcat[o * CH : (o + 1) * CH, :].astype(F32).T.astype(BF)
    step_exchange(2, 0, *first)

    def chain_up(j, last):
        face = slot_face[j]
        before = jnp.int32(0)
        for f in range(FACES):
            before = jnp.where(face == f, last[f], before)
        prev[j] = before
        return tuple(jnp.where(face == f, j + 1, last[f]) for f in range(FACES))

    last = lax.fori_loop(0, gn, chain_up, tuple(jnp.int32(0) for _ in range(FACES)))
    step_exchange(3, 0, *first)

    wait_for(flat(got_a), sems_a.at[1])
    for f in range(FACES):
        j = jnp.maximum(source[f], 0)
        taken = got_a[j // 8, lax.rem(j, 8)].astype(F32)
        ghost[f] = jnp.where(source[f] >= 0, taken, 0.0)

    build_views(cube, ghost, shifted, views)
    for b in range(2 * NB):
        rows = slice(b * VOX // 2, (b + 1) * VOX // 2)
        preact = product(views[rows, :], wcat[...])
        sigma = jax.nn.sigmoid(preact)
        flags = mask[rows, :]
        act_out[rows, :] = (flags * preact * sigma).astype(BF)
        delta = (cot[rows, :].astype(F32) * flags * sigma * (1.0 + preact * (1.0 - sigma))).astype(BF)
        cube[rows, :] = delta.astype(F32)
    cut_faces(cube, faces_b)
    start_exchange(faces_b, xc_n, *second)

    delta_t[...] = cube[...].T.astype(BF)
    for t in range(TAPS):
        csend[t * CH : (t + 1) * CH, :] = product(delta_t[...], views[:, t * CH : (t + 1) * CH]).T
    other = 1 - my_c
    twin = (z, at(my_x * CN + other, my_y))

    def half_of(ref, c):
        return ref.at[pl.ds(pl.multiple_of(c * half, 16), half)]

    send(half_of(csend, other), crecv, sems.at[6], sems.at[7], twin)
    wait_for(crecv, sems.at[7])
    total = half_of(csend, my_c)[...] + crecv[...]
    padding = jnp.zeros((zn, -share % 16, CH), F32)
    parts = jnp.concatenate([total.reshape(zn, share, CH), padding], axis=1)
    zsend[...] = parts.astype(BF)
    if zn > 1:
        repeat(1, zn, lambda k: send(
            zsend.at[z_peer(k)], zrecv.at[z], sems.at[8], sems.at[9], (z_peer(k), me)))
    zrecv[z] = zsend[z]
    step_exchange(1, xc_n, *second)
    if zn > 1:
        wait_for(zrecv.at[pl.ds(0, zn - 1)], sems.at[9])
    total = zrecv[0].astype(F32)
    for k in range(1, zn):
        total = total + zrecv[k].astype(F32)
    xgot[my_x] = total
    if XN > 1:
        repeat(1, XN, lambda k: send(
            xgot.at[my_x], xgot.at[my_x], sems.at[10], sems.at[11],
            (z, at(lax.rem(my_x + k, XN) * CN + my_c, my_y))))
    step_exchange(2, xc_n, *second)
    if XN > 1:
        wait_for(xgot.at[pl.ds(0, XN - 1)], sems.at[11])
    total = xgot[0]
    for k in range(1, XN):
        total = total + xgot[k]
    ygot[my_y] = total.astype(BF)
    repeat(1, YN, lambda k: send(
        ygot.at[my_y], ygot.at[my_y], sems.at[12], sems.at[13], (z, at(my_xc, wrap_y(k)))))
    step_exchange(3, xc_n, *second)
    wait_for(ygot.at[pl.ds(0, YN - 1)], sems.at[13])
    total = ygot[0].astype(F32)
    for k in range(1, YN):
        total = total + ygot[k].astype(F32)
    zgath[z] = total.astype(BF)
    if zn > 1:
        repeat(1, zn, lambda k: send(zgath.at[z], zgath.at[z], sems.at[14], sems.at[15], (z_peer(k), me)))

    wait_for(flat(got_b), sems_b.at[1])
    run[0] = jnp.zeros((64, CH), F32)

    def add_up(xc):
        for s in range(8):
            j = xc * 8 + s
            run[j + 1] = run[prev[j]] + got_b[xc, s].astype(F32)

    repeat(0, xc_n, add_up)
    for f in range(FACES):
        ghost[f] = run[last[f]]
    if zn > 1:
        wait_for(zgath.at[pl.ds(0, zn - 1)], sems.at[15])
    send(zgath, cgath, sems.at[16], sems.at[17], twin)
    build_views(cube, ghost, shifted, views)
    for b in range(2 * NB):
        rows = slice(b * VOX // 2, (b + 1) * VOX // 2)
        grad = product(views[rows, :], wback[...])
        grad_out[rows, :] = (mask[rows, :] * grad).astype(BF)

    wait_for(cgath, sems.at[17])
    half_of(wg_out, my_c)[...] = zgath[:, :share].astype(F32).reshape(half, CH) * scale
    half_of(wg_out, other)[...] = cgath[:, :share].astype(F32).reshape(half, CH) * scale

    drain(rows_a, up_a, down_a, chain_a, sems_a)
    drain(rows_b, up_b, down_b, chain_b, sems_b)
    wait_for(meta_out.at[pl.ds(0, 6)], sems.at[4])
    wait_for(crecv, sems.at[6])
    if zn > 1:
        wait_for(zsend.at[pl.ds(0, zn - 1)], sems.at[8])
        wait_for(zgath.at[pl.ds(0, zn - 1)], sems.at[14])
    if XN > 1:
        wait_for(xgot.at[pl.ds(0, XN - 1)], sems.at[10])
    wait_for(ygot.at[pl.ds(0, YN - 1)], sems.at[12])
    wait_for(zgath, sems.at[16])


def on_device(zn, gn, features, occupancy, weights, cotangent, send_count, send_face, recv_face):
    vmem = pl.BlockSpec(memory_space=pltpu.VMEM)
    anywhere = pl.BlockSpec(memory_space=pl.ANY)
    xc_n = XN * CN
    half = TAPS * CH // CN
    share = half // zn
    padded = -(-share // 16) * 16
    scale = float(zn * gn * ROWS) ** (-0.5)
    shells = [pltpu.VMEM((FACES, 64, CH), BF) for _ in range(3)]
    activated, grad, weight_grad = pl.pallas_call(
        functools.partial(kernel, zn, gn, scale),
        out_shape=(
            jax.ShapeDtypeStruct((ROWS, CH), BF),
            jax.ShapeDtypeStruct((ROWS, CH), BF),
            jax.ShapeDtypeStruct((TAPS * CH, CH), F32),
        ),
        in_specs=[anywhere] * 7,
        out_specs=(vmem, vmem, vmem),
        scratch_shapes=[
            pltpu.VMEM((ROWS, CH), BF),
            pltpu.VMEM((NB, VOX), jnp.int32),
            pltpu.VMEM((TAPS * CH, CH), BF),
            pltpu.VMEM((ROWS, CH), BF),
            pltpu.SMEM((gn,), jnp.int32),
            pltpu.SMEM((gn,), jnp.int32),
            pltpu.SMEM((gn,), jnp.int32),
            pltpu.VMEM((ROWS, CH), F32),
            pltpu.VMEM((ROWS, CH), F32),
            pltpu.VMEM((FACES, 64, CH), F32),
            pltpu.VMEM((VOX, CH), F32),
            pltpu.VMEM((ROWS, TAPS * CH), BF),
            pltpu.VMEM((TAPS * CH, CH), BF),
            pltpu.VMEM((CH, ROWS), BF),
            pltpu.VMEM((gn + 1, 64, CH), F32),
            pltpu.SMEM((gn,), jnp.int32),
            pltpu.SMEM((gn,), jnp.int32),
            pltpu.SMEM((gn,), jnp.int32),
            pltpu.SMEM((YN, 2 * xc_n), jnp.int32),
            pltpu.SMEM((YN, 2 * xc_n), jnp.int32),
            pltpu.VMEM((FACES, 64, CH), BF),
            pltpu.VMEM((FACES, 64, CH), BF),
            pltpu.VMEM((xc_n, 8, 64, CH), BF),
            pltpu.VMEM((xc_n, 8, 64, CH), BF),
            pltpu.VMEM((xc_n, 8, 64, CH), BF),
            pltpu.VMEM((xc_n, 8, 64, CH), BF),
            shells, shells, shells, shells,
            pltpu.VMEM((TAPS * CH, CH), F32),
            pltpu.VMEM((half, CH), F32),
            pltpu.VMEM((zn, padded, CH), BF),
            pltpu.VMEM((zn, padded, CH), BF),
            pltpu.VMEM((XN, padded, CH), F32),
            pltpu.VMEM((YN, padded, CH), BF),
            pltpu.VMEM((zn, padded, CH), BF),
            pltpu.VMEM((zn, padded, CH), BF),
            pltpu.SemaphoreType.DMA((7,)),
            pltpu.SemaphoreType.DMA((24,)),
            pltpu.SemaphoreType.DMA((24,)),
            pltpu.SemaphoreType.DMA((18,)),
        ],
        compiler_params=pltpu.CompilerParams(
            collective_id=0, has_side_effects=True, vmem_limit_bytes=40 * 1024 * 1024
        ),
        cost_estimate=pl.CostEstimate(
            flops=6 * ROWS * TAPS * CH * CH, bytes_accessed=2000000, transcendentals=ROWS * CH
        ),
    )(
        features.reshape(ROWS, CH),
        occupancy,
        weights.reshape(TAPS * CH, CH),
        cotangent.reshape(ROWS, CH),
        send_count.reshape(gn),
        send_face.reshape(gn),
        recv_face.reshape(gn),
    )
    return (
        activated.reshape(NB, VOX, CH),
        grad.reshape(NB, VOX, CH),
        weight_grad.reshape(TAPS, CH, CH),
    )


def solution(mesh):
    zn, gn = mesh.shape["gx"], mesh.shape["gy"]
    split = P(("gx", "gy"), None, None)
    return jax.shard_map(
        functools.partial(on_device, zn, gn),
        mesh=mesh,
        in_specs=(split, P(("gx", "gy"), None), P(), split, P(("gx", "gy"), None), split, split),
        out_specs=(split, split, P()),
        check_vma=False,
    )
```

```python
import functools

import jax
import jax.numpy as jnp
from jax import lax
from jax.experimental import pallas as pl
from jax.experimental.pallas import tpu as pltpu
from jax.sharding import PartitionSpec as P

XN = 4
YN = 8
CN = 2
MESH = pl.DeviceIdType.MESH
CH = 128
NB = 2
FACES = NB * 6
VOX = 512
ROWS = NB * VOX
TAPS = 7
OPPOSITE = (0, 2, 1, 4, 3, 6, 5)
BF = jnp.bfloat16
F32 = jnp.float32


def product(a, b):
    return jnp.dot(a, b, preferred_element_type=F32)


def cut_faces(cube, faces):
    for b in range(NB):
        base = b * VOX
        body = cube[base : base + VOX, :].reshape(8, 8, 8, CH)
        faces[b * 6 + 0] = cube[base : base + 64, :].astype(BF)
        faces[b * 6 + 1] = cube[base + 448 : base + 512, :].astype(BF)
        faces[b * 6 + 2] = body[:, 0].reshape(64, CH).astype(BF)
        faces[b * 6 + 3] = body[:, 7].reshape(64, CH).astype(BF)
        faces[b * 6 + 4] = cube[pl.ds(base, 64, stride=8), :].astype(BF)
        faces[b * 6 + 5] = cube[pl.ds(base + 7, 64, stride=8), :].astype(BF)


def build_views(cube, ghost, shifted, views):
    for b in range(NB):
        base = b * VOX
        rows = slice(base, base + VOX)
        g = b * 6
        body = cube[rows, :]
        solid = body.reshape(8, 8, 8, CH)
        views[rows, 0:128] = body.astype(BF)
        views[base : base + 64, 128:256] = ghost[g + 0].astype(BF)
        views[base + 64 : base + 512, 128:256] = cube[base : base + 448, :].astype(BF)
        views[base : base + 448, 256:384] = cube[base + 64 : base + 512, :].astype(BF)
        views[base + 448 : base + 512, 256:384] = ghost[g + 1].astype(BF)
        low = ghost[g + 2].reshape(8, 1, 8, CH)
        high = ghost[g + 3].reshape(8, 1, 8, CH)
        views[rows, 384:512] = jnp.concatenate([low, solid[:, :7]], axis=1).reshape(VOX, CH).astype(BF)
        views[rows, 512:640] = jnp.concatenate([solid[:, 1:], high], axis=1).reshape(VOX, CH).astype(BF)
        shifted[1:VOX, :] = cube[base : base + VOX - 1, :]
        shifted[pl.ds(0, 64, stride=8), :] = ghost[g + 4]
        views[rows, 640:768] = shifted[...].astype(BF)
        shifted[0 : VOX - 1, :] = cube[base + 1 : base + VOX, :]
        shifted[pl.ds(7, 64, stride=8), :] = ghost[g + 5]
        views[rows, 768:896] = shifted[...].astype(BF)


ROW_OF = (0, 4, -1, 1, -2, 2, -3, 3)
PIECES = 3


def kernel(
    zn, gn, scale,
    feat_in, occ_in, wcat_in, cot_in, count_in, sface_in, rface_in,
    act_out, grad_out, wg_out,
    feat, occ, wcat, cot, count, sface, rface,
    mask, cube, ghost, shifted, views, wback, delta_t, run, prev, slot_face, slot_row, meta_out, meta_in, meta_far,
    faces_a, faces_b, rows_a, rows_b, got_a, got_b, up_a, down_a, up_b, down_b,
    csend, crecv, zsend, zrecv, xgot, ygot, zgath, cgath,
    load_sems, chain_a, chain_b, sems,
):
    z = lax.axis_index("gx")
    me = lax.axis_index("gy")
    xc_n = XN * CN
    my_x = me // (YN * CN)
    my_y = lax.rem(me // CN, YN)
    my_c = lax.rem(me, CN)
    my_xc = my_x * CN + my_c
    half = TAPS * CH // CN
    share = half // zn

    def wrap_y(offset):
        return lax.rem(my_y + offset + YN, YN)

    def at(xc, y):
        return (xc // CN * YN + y) * CN + lax.rem(xc, CN)

    def xc_peer(k):
        return lax.rem(my_xc + k, xc_n)

    def z_peer(k):
        return lax.rem(z + k, zn)

    def repeat(low, high, body):
        def step(i, _):
            body(i)
            return 0

        lax.fori_loop(low, high, step, 0)

    def send(src, dst, send_sem, recv_sem, to):
        copy = pltpu.make_async_remote_copy(
            src_ref=src, dst_ref=dst, send_sem=send_sem, recv_sem=recv_sem, device_id=to, device_id_type=MESH
        )
        copy.start()

    def wait_for(ref, sem):
        pltpu.make_async_copy(ref, ref, sem).wait()

    barrier = pltpu.get_barrier_semaphore()

    def greet(to):
        pl.semaphore_signal(barrier, inc=1, device_id=to, device_id_type=MESH)

    repeat(1, YN, lambda k: greet((z, at(my_xc, wrap_y(k)))))
    repeat(1, xc_n, lambda k: greet((z, at(xc_peer(k), my_y))))
    repeat(1, xc_n, lambda k: greet((z, at(xc_peer(k), wrap_y(1)))))
    repeat(1, xc_n, lambda k: greet((z, at(xc_peer(k), wrap_y(-1)))))
    if zn > 1:
        repeat(1, zn, lambda k: greet((z_peer(k), me)))

    loads = [
        pltpu.make_async_copy(src, dst, load_sems.at[i])
        for i, (src, dst) in enumerate(
            [(occ_in, occ), (feat_in, feat), (sface_in, sface), (rface_in, rface), (count_in, count), (wcat_in, wcat),
             (cot_in, cot)]
        )
    ]
    for load in loads:
        load.start()

    diagonal = lax.broadcasted_iota(jnp.int32, (CH, CH), 0) == lax.broadcasted_iota(jnp.int32, (CH, CH), 1)
    ones = jnp.ones((CH, CH), BF)
    loads[0].wait()
    loads[1].wait()
    for b in range(NB):
        for i in range(VOX // CH):
            row = (occ[b : b + 1, i * CH : (i + 1) * CH] > 0).astype(F32)
            spread = jnp.where(diagonal, jnp.broadcast_to(row, (CH, CH)), 0.0).astype(BF)
            place = b * VOX + i * CH
            flags = product(spread, ones)
            mask[place : place + CH, :] = flags
            cube[place : place + CH, :] = jnp.where(flags > 0, feat[place : place + CH, :].astype(F32), 0.0)
    cut_faces(cube, faces_a)
    loads[2].wait()
    loads[3].wait()
    loads[4].wait()

    def fill_meta(y):
        for xc in range(xc_n):
            meta_out[y, xc] = sface[at(jnp.int32(xc), y)]
            meta_out[y, xc_n + xc] = jnp.maximum(rface[at(jnp.int32(xc), y)], 0)

    repeat(0, YN, fill_meta)

    def start_exchange(faces, column, rows, got, up, down, chain, row_sems):
        for p in range(PIECES):
            part = pl.ds(p * 4, 4)
            send(faces.at[part], up[0].at[part], chain.at[0], chain.at[6 + p], (z, at(my_xc, wrap_y(1))))
            send(faces.at[part], down[0].at[part], chain.at[3], chain.at[6 + 9 + p], (z, at(my_xc, wrap_y(-1))))

        def pick(xc):
            rows[xc, 0] = faces[meta_out[my_y, column + xc]]

        repeat(0, xc_n, pick)

        def ship_own(k):
            xc = xc_peer(k)
            send(rows.at[xc, 0], got.at[my_xc, 0], row_sems.at[0], row_sems.at[1], (z, at(xc, my_y)))

        repeat(1, xc_n, ship_own)
        got[my_xc, 0] = rows[my_xc, 0]

    def step_exchange(d, column, rows, got, up, down, chain, row_sems):
        for p in range(PIECES):
            part = pl.ds(p * 4, 4)
            wait_for(up[d - 1].at[part], chain.at[6 + (d - 1) * 3 + p])
            if d < 3:
                send(up[d - 1].at[part], up[d].at[part], chain.at[d], chain.at[6 + d * 3 + p],
                     (z, at(my_xc, wrap_y(1))))
            wait_for(down[d - 1].at[part], chain.at[6 + 9 + (d - 1) * 3 + p])
            if d < 3:
                send(down[d - 1].at[part], down[d].at[part], chain.at[3 + d], chain.at[6 + 9 + d * 3 + p],
                     (z, at(my_xc, wrap_y(-1))))
        low, high = wrap_y(-d), wrap_y(d)

        def pick(xc):
            rows[xc, 2 * d] = up[d - 1][meta_in[low, column + xc]]
            rows[xc, 2 * d + 1] = down[d - 1][meta_in[high, column + xc]]

        repeat(0, xc_n, pick)
        pair = pl.ds(2 * d, 2)
        if d == 3:
            def pick_up(xc):
                rows[xc, 1] = up[2][meta_far[low, column + xc]]
                send(rows.at[xc, 1], got.at[my_xc, 1], row_sems.at[0], row_sems.at[1], (z, at(xc, wrap_y(1))))

            def pick_down(xc):
                rows[xc, 1] = down[2][meta_far[high, column + xc]]
                send(rows.at[xc, 1], got.at[my_xc, 1], row_sems.at[0], row_sems.at[1], (z, at(xc, wrap_y(-1))))

            repeat(0, xc_n // 2, pick_up)
            repeat(xc_n // 2, xc_n, pick_down)

        def ship(k):
            xc = xc_peer(k)
            send(rows.at[xc, pair], got.at[my_xc, pair], row_sems.at[0], row_sems.at[1], (z, at(xc, my_y)))

        repeat(1, xc_n, ship)
        got[my_xc, pair] = rows[my_xc, pair]

    remote_faces = (xc_n - 1) * 7 + xc_n

    def flat(ref):
        return ref.reshape(xc_n * 8, 64, CH).at[pl.ds(0, remote_faces)]

    def drain(rows, up, down, chain, row_sems):
        for d in range(3):
            wait_for(up[d], chain.at[d])
            wait_for(down[d], chain.at[3 + d])
        wait_for(flat(rows), row_sems.at[0])

    pl.semaphore_wait(barrier, (YN - 1) + 3 * (xc_n - 1) + (zn - 1))
    sems_a, sems_b = sems.at[pl.ds(0, 2)], sems.at[pl.ds(2, 2)]
    for d in (1, -1, 2, -2, 3, -3):
        y = wrap_y(d)
        send(meta_out.at[y], meta_in.at[my_y], sems.at[4], sems.at[5], (z, at(my_xc, y)))
    for d in (3, -3):
        send(meta_out.at[wrap_y(4)], meta_far.at[my_y], sems.at[18], sems.at[19], (z, at(my_xc, wrap_y(d))))
    first = (rows_a, got_a, up_a, down_a, chain_a, sems_a)
    second = (rows_b, got_b, up_b, down_b, chain_b, sems_b)
    start_exchange(faces_a, 0, *first)

    def list_slots(xc):
        for s in range(8):
            p = at(xc, wrap_y(ROW_OF[s]))
            slot_row[xc * 8 + s] = rface[p]
            slot_face[xc * 8 + s] = jnp.where(count[p] > 0, sface[p], FACES)

    repeat(0, xc_n, list_slots)

    def find_source(j, found):
        row = slot_row[j]
        return tuple(jnp.where(row == f, j, found[f]) for f in range(FACES))

    source = lax.fori_loop(0, gn, find_source, tuple(jnp.int32(-1) for _ in range(FACES)))
    loads[5].wait()
    loads[6].wait()
    wait_for(meta_in.at[pl.ds(0, 6)], sems.at[5])
    step_exchange(1, 0, *first)
    for t in range(TAPS):
        o = OPPOSITE[t]
        wback[t * CH : (t + 1) * CH, :] = wcat[o * CH : (o + 1) * CH, :].astype(F32).T.astype(BF)
    step_exchange(2, 0, *first)

    def chain_up(j, last):
        face = slot_face[j]
        before = jnp.int32(0)
        for f in range(FACES):
            before = jnp.where(face == f, last[f], before)
        prev[j] = before
        return tuple(jnp.where(face == f, j + 1, last[f]) for f in range(FACES))

    last = lax.fori_loop(0, gn, chain_up, tuple(jnp.int32(0) for _ in range(FACES)))
    wait_for(meta_far.at[pl.ds(0, 2)], sems.at[19])
    step_exchange(3, 0, *first)

    wait_for(flat(got_a), sems_a.at[1])
    for f in range(FACES):
        j = jnp.maximum(source[f], 0)
        taken = got_a[j // 8, lax.rem(j, 8)].astype(F32)
        ghost[f] = jnp.where(source[f] >= 0, taken, 0.0)

    build_views(cube, ghost, shifted, views)
    for b in range(2 * NB):
        rows = slice(b * VOX // 2, (b + 1) * VOX // 2)
        preact = product(views[rows, :], wcat[...])
        sigma = jax.nn.sigmoid(preact)
        flags = mask[rows, :]
        act_out[rows, :] = (flags * preact * sigma).astype(BF)
        delta = (cot[rows, :].astype(F32) * flags * sigma * (1.0 + preact * (1.0 - sigma))).astype(BF)
        cube[rows, :] = delta.astype(F32)
    cut_faces(cube, faces_b)
    start_exchange(faces_b, xc_n, *second)

    delta_t[...] = cube[...].T.astype(BF)
    for t in range(TAPS):
        csend[t * CH : (t + 1) * CH, :] = product(delta_t[...], views[:, t * CH : (t + 1) * CH]).T
    other = 1 - my_c
    twin = (z, at(my_x * CN + other, my_y))

    def half_of(ref, c):
        return ref.at[pl.ds(pl.multiple_of(c * half, 16), half)]

    send(half_of(csend, other), crecv, sems.at[6], sems.at[7], twin)
    wait_for(crecv, sems.at[7])
    total = half_of(csend, my_c)[...] + crecv[...]
    padding = jnp.zeros((zn, -share % 16, CH), F32)
    parts = jnp.concatenate([total.reshape(zn, share, CH), padding], axis=1)
    zsend[...] = parts.astype(BF)
    if zn > 1:
        repeat(1, zn, lambda k: send(
            zsend.at[z_peer(k)], zrecv.at[z], sems.at[8], sems.at[9], (z_peer(k), me)))
    zrecv[z] = zsend[z]
    step_exchange(1, xc_n, *second)
    step_exchange(2, xc_n, *second)
    if zn > 1:
        wait_for(zrecv.at[pl.ds(0, zn - 1)], sems.at[9])
    total = zrecv[0].astype(F32)
    for k in range(1, zn):
        total = total + zrecv[k].astype(F32)
    xgot[my_x] = total
    if XN > 1:
        repeat(1, XN, lambda k: send(
            xgot.at[my_x], xgot.at[my_x], sems.at[10], sems.at[11],
            (z, at(lax.rem(my_x + k, XN) * CN + my_c, my_y))))
    if XN > 1:
        wait_for(xgot.at[pl.ds(0, XN - 1)], sems.at[11])
    total = xgot[0]
    for k in range(1, XN):
        total = total + xgot[k]
    ygot[my_y] = total.astype(BF)
    repeat(1, YN, lambda k: send(
        ygot.at[my_y], ygot.at[my_y], sems.at[12], sems.at[13], (z, at(my_xc, wrap_y(k)))))
    step_exchange(3, xc_n, *second)
    wait_for(ygot.at[pl.ds(0, YN - 1)], sems.at[13])
    total = ygot[0].astype(F32)
    for k in range(1, YN):
        total = total + ygot[k].astype(F32)
    zgath[z] = total.astype(BF)
    if zn > 1:
        repeat(1, zn, lambda k: send(zgath.at[z], zgath.at[z], sems.at[14], sems.at[15], (z_peer(k), me)))

    wait_for(flat(got_b), sems_b.at[1])
    run[0] = jnp.zeros((64, CH), F32)

    def add_up(xc):
        for s in range(8):
            j = xc * 8 + s
            run[j + 1] = run[prev[j]] + got_b[xc, s].astype(F32)

    repeat(0, xc_n, add_up)
    for f in range(FACES):
        ghost[f] = run[last[f]]
    if zn > 1:
        wait_for(zgath.at[pl.ds(0, zn - 1)], sems.at[15])
    send(zgath, cgath, sems.at[16], sems.at[17], twin)
    build_views(cube, ghost, shifted, views)
    for b in range(2 * NB):
        rows = slice(b * VOX // 2, (b + 1) * VOX // 2)
        grad = product(views[rows, :], wback[...])
        grad_out[rows, :] = (mask[rows, :] * grad).astype(BF)

    wait_for(cgath, sems.at[17])
    half_of(wg_out, my_c)[...] = zgath[:, :share].astype(F32).reshape(half, CH) * scale
    half_of(wg_out, other)[...] = cgath[:, :share].astype(F32).reshape(half, CH) * scale

    drain(rows_a, up_a, down_a, chain_a, sems_a)
    drain(rows_b, up_b, down_b, chain_b, sems_b)
    wait_for(meta_out.at[pl.ds(0, 6)], sems.at[4])
    wait_for(meta_out.at[pl.ds(0, 2)], sems.at[18])
    wait_for(crecv, sems.at[6])
    if zn > 1:
        wait_for(zsend.at[pl.ds(0, zn - 1)], sems.at[8])
        wait_for(zgath.at[pl.ds(0, zn - 1)], sems.at[14])
    if XN > 1:
        wait_for(xgot.at[pl.ds(0, XN - 1)], sems.at[10])
    wait_for(ygot.at[pl.ds(0, YN - 1)], sems.at[12])
    wait_for(zgath, sems.at[16])


def on_device(zn, gn, features, occupancy, weights, cotangent, send_count, send_face, recv_face):
    vmem = pl.BlockSpec(memory_space=pltpu.VMEM)
    anywhere = pl.BlockSpec(memory_space=pltpu.HBM)
    xc_n = XN * CN
    half = TAPS * CH // CN
    share = half // zn
    padded = -(-share // 16) * 16
    scale = float(zn * gn * ROWS) ** (-0.5)
    shells = [pltpu.VMEM((FACES, 64, CH), BF) for _ in range(3)]
    activated, grad, weight_grad = pl.pallas_call(
        functools.partial(kernel, zn, gn, scale),
        out_shape=(
            jax.ShapeDtypeStruct((ROWS, CH), BF),
            jax.ShapeDtypeStruct((ROWS, CH), BF),
            jax.ShapeDtypeStruct((TAPS * CH, CH), F32),
        ),
        in_specs=[anywhere] * 7,
        out_specs=(vmem, vmem, vmem),
        scratch_shapes=[
            pltpu.VMEM((ROWS, CH), BF),
            pltpu.VMEM((NB, VOX), jnp.int32),
            pltpu.VMEM((TAPS * CH, CH), BF),
            pltpu.VMEM((ROWS, CH), BF),
            pltpu.SMEM((gn,), jnp.int32),
            pltpu.SMEM((gn,), jnp.int32),
            pltpu.SMEM((gn,), jnp.int32),
            pltpu.VMEM((ROWS, CH), F32),
            pltpu.VMEM((ROWS, CH), F32),
            pltpu.VMEM((FACES, 64, CH), F32),
            pltpu.VMEM((VOX, CH), F32),
            pltpu.VMEM((ROWS, TAPS * CH), BF),
            pltpu.VMEM((TAPS * CH, CH), BF),
            pltpu.VMEM((CH, ROWS), BF),
            pltpu.VMEM((gn + 1, 64, CH), F32),
            pltpu.SMEM((gn,), jnp.int32),
            pltpu.SMEM((gn,), jnp.int32),
            pltpu.SMEM((gn,), jnp.int32),
            pltpu.SMEM((YN, 2 * xc_n), jnp.int32),
            pltpu.SMEM((YN, 2 * xc_n), jnp.int32),
            pltpu.SMEM((YN, 2 * xc_n), jnp.int32),
            pltpu.VMEM((FACES, 64, CH), BF),
            pltpu.VMEM((FACES, 64, CH), BF),
            pltpu.VMEM((xc_n, 8, 64, CH), BF),
            pltpu.VMEM((xc_n, 8, 64, CH), BF),
            pltpu.VMEM((xc_n, 8, 64, CH), BF),
            pltpu.VMEM((xc_n, 8, 64, CH), BF),
            shells, shells, shells, shells,
            pltpu.VMEM((TAPS * CH, CH), F32),
            pltpu.VMEM((half, CH), F32),
            pltpu.VMEM((zn, padded, CH), BF),
            pltpu.VMEM((zn, padded, CH), BF),
            pltpu.VMEM((XN, padded, CH), F32),
            pltpu.VMEM((YN, padded, CH), BF),
            pltpu.VMEM((zn, padded, CH), BF),
            pltpu.VMEM((zn, padded, CH), BF),
            pltpu.SemaphoreType.DMA((7,)),
            pltpu.SemaphoreType.DMA((24,)),
            pltpu.SemaphoreType.DMA((24,)),
            pltpu.SemaphoreType.DMA((20,)),
        ],
        compiler_params=pltpu.CompilerParams(
            collective_id=0, has_side_effects=True, vmem_limit_bytes=62 * 1024 * 1024
        ),
        cost_estimate=pl.CostEstimate(
            flops=6 * ROWS * TAPS * CH * CH, bytes_accessed=2000000, transcendentals=ROWS * CH
        ),
    )(
        features.reshape(ROWS, CH),
        occupancy,
        weights.reshape(TAPS * CH, CH),
        cotangent.reshape(ROWS, CH),
        send_count.reshape(gn),
        send_face.reshape(gn),
        recv_face.reshape(gn),
    )
    return (
        activated.reshape(NB, VOX, CH),
        grad.reshape(NB, VOX, CH),
        weight_grad.reshape(TAPS, CH, CH),
    )


def solution(mesh):
    zn, gn = mesh.shape["gx"], mesh.shape["gy"]
    split = P(("gx", "gy"), None, None)
    return jax.shard_map(
        functools.partial(on_device, zn, gn),
        mesh=mesh,
        in_specs=(split, P(("gx", "gy"), None), P(), split, P(("gx", "gy"), None), split, split),
        out_specs=(split, split, P()),
        check_vma=False,
    )
```

```python
import functools

import jax
import jax.numpy as jnp
from jax import lax
from jax.experimental import pallas as pl
from jax.experimental.pallas import tpu as pltpu
from jax.sharding import PartitionSpec as P

XN = 4
YN = 8
CN = 2
MESH = pl.DeviceIdType.MESH
CH = 128
NB = 2
FACES = NB * 6
VOX = 512
ROWS = NB * VOX
TAPS = 7
OPPOSITE = (0, 2, 1, 4, 3, 6, 5)
BF = jnp.bfloat16
F32 = jnp.float32


def product(a, b):
    return jnp.dot(a, b, preferred_element_type=F32)


def cut_faces(cube, faces):
    for b in range(NB):
        base = b * VOX
        body = cube[base : base + VOX, :].reshape(8, 8, 8, CH)
        faces[b * 6 + 0] = cube[base : base + 64, :].astype(BF)
        faces[b * 6 + 1] = cube[base + 448 : base + 512, :].astype(BF)
        faces[b * 6 + 2] = body[:, 0].reshape(64, CH).astype(BF)
        faces[b * 6 + 3] = body[:, 7].reshape(64, CH).astype(BF)
        faces[b * 6 + 4] = cube[pl.ds(base, 64, stride=8), :].astype(BF)
        faces[b * 6 + 5] = cube[pl.ds(base + 7, 64, stride=8), :].astype(BF)


def build_views(cube, ghost, shifted, views):
    for b in range(NB):
        base = b * VOX
        rows = slice(base, base + VOX)
        g = b * 6
        body = cube[rows, :]
        solid = body.reshape(8, 8, 8, CH)
        views[rows, 0:128] = body.astype(BF)
        views[base : base + 64, 128:256] = ghost[g + 0].astype(BF)
        views[base + 64 : base + 512, 128:256] = cube[base : base + 448, :].astype(BF)
        views[base : base + 448, 256:384] = cube[base + 64 : base + 512, :].astype(BF)
        views[base + 448 : base + 512, 256:384] = ghost[g + 1].astype(BF)
        low = ghost[g + 2].reshape(8, 1, 8, CH)
        high = ghost[g + 3].reshape(8, 1, 8, CH)
        views[rows, 384:512] = jnp.concatenate([low, solid[:, :7]], axis=1).reshape(VOX, CH).astype(BF)
        views[rows, 512:640] = jnp.concatenate([solid[:, 1:], high], axis=1).reshape(VOX, CH).astype(BF)
        shifted[1:VOX, :] = cube[base : base + VOX - 1, :]
        shifted[pl.ds(0, 64, stride=8), :] = ghost[g + 4]
        views[rows, 640:768] = shifted[...].astype(BF)
        shifted[0 : VOX - 1, :] = cube[base + 1 : base + VOX, :]
        shifted[pl.ds(7, 64, stride=8), :] = ghost[g + 5]
        views[rows, 768:896] = shifted[...].astype(BF)


ROW_OF = (0, 4, -1, 1, -2, 2, -3, 3)
PIECES = 3


def kernel(
    zn, gn,
    feat_in, occ_in, wcat_in, cot_in, count_in, sface_in, rface_in,
    act_out, grad_out, wg_out,
    feat, occ, wcat, cot, count, sface, rface,
    mask, cube, ghost, shifted, views, wback, delta_t, run, prev, slot_face, slot_row, meta_out, meta_in, meta_far,
    faces_a, faces_b, rows_a, rows_b, got_a, got_b, up_a, down_a, up_b, down_b,
    csend, crecv, zsend, zrecv, ygot, zgath, cgath, act, grad,
    load_sems, out_sems, chain_a, chain_b, sems,
):
    z = lax.axis_index("gx")
    me = lax.axis_index("gy")
    xc_n = XN * CN
    my_x = me // (YN * CN)
    my_y = lax.rem(me // CN, YN)
    my_c = lax.rem(me, CN)
    my_xc = my_x * CN + my_c
    half = TAPS * CH // CN
    en = zn * XN
    me_e = z * XN + my_x
    piece = zrecv.shape[1]

    def wrap_y(offset):
        return lax.rem(my_y + offset + YN, YN)

    def at(xc, y):
        return (xc // CN * YN + y) * CN + lax.rem(xc, CN)

    def xc_peer(k):
        return lax.rem(my_xc + k, xc_n)

    def zx_peer(k):
        return lax.rem(me_e + k, en)

    def zx_device(e):
        return (e // XN, at(lax.rem(e, XN) * CN + my_c, my_y))

    def repeat(low, high, body):
        def step(i, _):
            body(i)
            return 0

        lax.fori_loop(low, high, step, 0)

    def send(src, dst, send_sem, recv_sem, to):
        copy = pltpu.make_async_remote_copy(
            src_ref=src, dst_ref=dst, send_sem=send_sem, recv_sem=recv_sem, device_id=to, device_id_type=MESH
        )
        copy.start()

    def wait_for(ref, sem):
        pltpu.make_async_copy(ref, ref, sem).wait()

    barrier = pltpu.get_barrier_semaphore()

    def greet(to):
        pl.semaphore_signal(barrier, inc=1, device_id=to, device_id_type=MESH)

    repeat(1, YN, lambda k: greet((z, at(my_xc, wrap_y(k)))))
    repeat(1, xc_n, lambda k: greet((z, at(xc_peer(k), my_y))))
    repeat(1, xc_n, lambda k: greet((z, at(xc_peer(k), wrap_y(1)))))
    repeat(1, xc_n, lambda k: greet((z, at(xc_peer(k), wrap_y(-1)))))
    repeat(XN, en, lambda k: greet(zx_device(lax.rem(z * XN + k, en))))

    loads = [
        pltpu.make_async_copy(src, dst, load_sems.at[i])
        for i, (src, dst) in enumerate(
            [(occ_in, occ), (feat_in, feat), (sface_in, sface), (rface_in, rface), (count_in, count), (wcat_in, wcat),
             (cot_in, cot)]
        )
    ]
    for load in loads:
        load.start()

    diagonal = lax.broadcasted_iota(jnp.int32, (CH, CH), 0) == lax.broadcasted_iota(jnp.int32, (CH, CH), 1)
    ones = jnp.ones((CH, CH), BF)
    loads[0].wait()
    loads[1].wait()
    for b in range(NB):
        for i in range(VOX // CH):
            row = (occ[b : b + 1, i * CH : (i + 1) * CH] > 0).astype(F32)
            spread = jnp.where(diagonal, jnp.broadcast_to(row, (CH, CH)), 0.0).astype(BF)
            place = b * VOX + i * CH
            flags = product(spread, ones)
            mask[place : place + CH, :] = flags
            cube[place : place + CH, :] = jnp.where(flags > 0, feat[place : place + CH, :].astype(F32), 0.0)
    cut_faces(cube, faces_a)
    loads[2].wait()
    loads[3].wait()
    loads[4].wait()

    def fill_meta(y):
        for xc in range(xc_n):
            meta_out[y, xc] = sface[at(jnp.int32(xc), y)]
            meta_out[y, xc_n + xc] = jnp.maximum(rface[at(jnp.int32(xc), y)], 0)

    repeat(0, YN, fill_meta)

    def start_exchange(faces, column, rows, got, up, down, chain, row_sems):
        for p in range(PIECES):
            part = pl.ds(p * 4, 4)
            send(faces.at[part], up[0].at[part], chain.at[0], chain.at[6 + p], (z, at(my_xc, wrap_y(1))))
            send(faces.at[part], down[0].at[part], chain.at[3], chain.at[6 + 9 + p], (z, at(my_xc, wrap_y(-1))))

        def pick(xc):
            rows[xc, 0] = faces[meta_out[my_y, column + xc]]

        repeat(0, xc_n, pick)

        def ship_own(k):
            xc = xc_peer(k)
            send(rows.at[xc, 0], got.at[my_xc, 0], row_sems.at[0], row_sems.at[1], (z, at(xc, my_y)))

        repeat(1, xc_n, ship_own)
        got[my_xc, 0] = rows[my_xc, 0]

    def step_exchange(d, column, rows, got, up, down, chain, row_sems):
        for p in range(PIECES):
            part = pl.ds(p * 4, 4)
            wait_for(up[d - 1].at[part], chain.at[6 + (d - 1) * 3 + p])
            if d < 3:
                send(up[d - 1].at[part], up[d].at[part], chain.at[d], chain.at[6 + d * 3 + p],
                     (z, at(my_xc, wrap_y(1))))
            wait_for(down[d - 1].at[part], chain.at[6 + 9 + (d - 1) * 3 + p])
            if d < 3:
                send(down[d - 1].at[part], down[d].at[part], chain.at[3 + d], chain.at[6 + 9 + d * 3 + p],
                     (z, at(my_xc, wrap_y(-1))))
        low, high = wrap_y(-d), wrap_y(d)

        def pick(xc):
            rows[xc, 2 * d] = up[d - 1][meta_in[low, column + xc]]
            rows[xc, 2 * d + 1] = down[d - 1][meta_in[high, column + xc]]

        repeat(0, xc_n, pick)
        pair = pl.ds(2 * d, 2)
        if d == 3:
            def pick_up(xc):
                rows[xc, 1] = up[2][meta_far[low, column + xc]]
                send(rows.at[xc, 1], got.at[my_xc, 1], row_sems.at[0], row_sems.at[1], (z, at(xc, wrap_y(1))))

            def pick_down(xc):
                rows[xc, 1] = down[2][meta_far[high, column + xc]]
                send(rows.at[xc, 1], got.at[my_xc, 1], row_sems.at[0], row_sems.at[1], (z, at(xc, wrap_y(-1))))

            repeat(0, xc_n // 2, pick_up)
            repeat(xc_n // 2, xc_n, pick_down)

        def ship(k):
            xc = xc_peer(k)
            send(rows.at[xc, pair], got.at[my_xc, pair], row_sems.at[0], row_sems.at[1], (z, at(xc, my_y)))

        repeat(1, xc_n, ship)
        got[my_xc, pair] = rows[my_xc, pair]

    remote_faces = (xc_n - 1) * 7 + xc_n

    def flat(ref):
        return ref.reshape(xc_n * 8, 64, CH).at[pl.ds(0, remote_faces)]

    def drain(rows, up, down, chain, row_sems):
        for d in range(3):
            wait_for(up[d], chain.at[d])
            wait_for(down[d], chain.at[3 + d])
        wait_for(flat(rows), row_sems.at[0])

    pl.semaphore_wait(barrier, (YN - 1) + 3 * (xc_n - 1) + (zn - 1) * XN)
    sems_a, sems_b = sems.at[pl.ds(0, 2)], sems.at[pl.ds(2, 2)]
    for d in (1, -1, 2, -2, 3, -3):
        y = wrap_y(d)
        send(meta_out.at[y], meta_in.at[my_y], sems.at[4], sems.at[5], (z, at(my_xc, y)))
    for d in (3, -3):
        send(meta_out.at[wrap_y(4)], meta_far.at[my_y], sems.at[18], sems.at[19], (z, at(my_xc, wrap_y(d))))
    first = (rows_a, got_a, up_a, down_a, chain_a, sems_a)
    second = (rows_b, got_b, up_b, down_b, chain_b, sems_b)
    start_exchange(faces_a, 0, *first)

    wait_for(meta_in.at[pl.ds(0, 6)], sems.at[5])
    step_exchange(1, 0, *first)
    step_exchange(2, 0, *first)

    wait_for(meta_far.at[pl.ds(0, 2)], sems.at[19])
    step_exchange(3, 0, *first)

    def list_slots(xc):
        for s in range(8):
            p = at(xc, wrap_y(ROW_OF[s]))
            slot_row[xc * 8 + s] = rface[p]
            slot_face[xc * 8 + s] = jnp.where(count[p] > 0, sface[p], FACES)

    repeat(0, xc_n, list_slots)

    def find_source(j, found):
        row = slot_row[j]
        return tuple(jnp.where(row == f, j, found[f]) for f in range(FACES))

    source = lax.fori_loop(0, gn, find_source, tuple(jnp.int32(-1) for _ in range(FACES)))
    def chain_up(j, last):
        face = slot_face[j]
        before = jnp.int32(0)
        for f in range(FACES):
            before = jnp.where(face == f, last[f], before)
        prev[j] = before
        return tuple(jnp.where(face == f, j + 1, last[f]) for f in range(FACES))

    last = lax.fori_loop(0, gn, chain_up, tuple(jnp.int32(0) for _ in range(FACES)))
    loads[5].wait()
    loads[6].wait()
    for t in range(TAPS):
        o = OPPOSITE[t]
        wback[t * CH : (t + 1) * CH, :] = wcat[o * CH : (o + 1) * CH, :].astype(F32).T.astype(BF)

    wait_for(flat(got_a), sems_a.at[1])
    for f in range(FACES):
        j = jnp.maximum(source[f], 0)
        taken = got_a[j // 8, lax.rem(j, 8)].astype(F32)
        ghost[f] = jnp.where(source[f] >= 0, taken, 0.0)

    build_views(cube, ghost, shifted, views)
    for b in range(2 * NB):
        rows = slice(b * VOX // 2, (b + 1) * VOX // 2)
        preact = product(views[rows, :], wcat[...])
        sigma = jax.nn.sigmoid(preact)
        flags = mask[rows, :]
        act[rows, :] = (flags * preact * sigma).astype(BF)
        delta = (cot[rows, :].astype(F32) * flags * sigma * (1.0 + preact * (1.0 - sigma))).astype(BF)
        cube[rows, :] = delta.astype(F32)
    cut_faces(cube, faces_b)
    start_exchange(faces_b, xc_n, *second)
    store_act = pltpu.make_async_copy(act, act_out, out_sems.at[0])
    store_act.start()

    delta_t[...] = cube[...].T.astype(BF)
    for t in range(TAPS):
        csend[t * CH : (t + 1) * CH, :] = product(delta_t[...], views[:, t * CH : (t + 1) * CH]).T
    other = 1 - my_c
    twin = (z, at(my_x * CN + other, my_y))

    def half_of(ref, c):
        return ref.at[pl.ds(pl.multiple_of(c * half, 16), half)]

    send(half_of(csend, other), crecv, sems.at[6], sems.at[7], twin)
    wait_for(crecv, sems.at[7])
    total = half_of(csend, my_c)[...] + crecv[...]
    zsend[0:half, :] = total.astype(BF)
    if en * piece > half:
        zsend[half:, :] = jnp.zeros((en * piece - half, CH), BF)

    def piece_of(ref, e):
        return ref.at[pl.ds(pl.multiple_of(e * piece, 16), piece)]

    def scatter(k):
        e = zx_peer(k)
        send(piece_of(zsend, e), zrecv.at[me_e], sems.at[8], sems.at[9], zx_device(e))

    repeat(1, en, scatter)
    zrecv[me_e] = piece_of(zsend, me_e)[...]
    step_exchange(1, xc_n, *second)
    step_exchange(2, xc_n, *second)
    wait_for(zrecv.at[pl.ds(0, en - 1)], sems.at[9])
    ygot[my_y] = jnp.sum(zrecv[...].astype(F32), axis=0)
    repeat(1, YN, lambda k: send(
        ygot.at[my_y], ygot.at[my_y], sems.at[12], sems.at[13], (z, at(my_xc, wrap_y(k)))))
    step_exchange(3, xc_n, *second)
    wait_for(ygot.at[pl.ds(0, YN - 1)], sems.at[13])
    total = ygot[0]
    for k in range(1, YN):
        total = total + ygot[k]
    mine = piece_of(zgath, me_e)
    mine[...] = total.astype(BF)
    repeat(1, en, lambda k: send(mine, mine, sems.at[14], sems.at[15], zx_device(zx_peer(k))))

    wait_for(flat(got_b), sems_b.at[1])
    run[0] = jnp.zeros((64, CH), F32)

    def add_up(xc):
        for s in range(8):
            j = xc * 8 + s
            run[j + 1] = run[prev[j]] + got_b[xc, s].astype(F32)

    repeat(0, xc_n, add_up)
    for f in range(FACES):
        ghost[f] = run[last[f]]
    wait_for(zgath.at[pl.ds(0, (en - 1) * piece)], sems.at[15])
    send(zgath.at[pl.ds(0, half)], cgath, sems.at[16], sems.at[17], twin)
    build_views(cube, ghost, shifted, views)
    for b in range(2 * NB):
        rows = slice(b * VOX // 2, (b + 1) * VOX // 2)
        grad[rows, :] = (mask[rows, :] * product(views[rows, :], wback[...])).astype(BF)

    store_grad = pltpu.make_async_copy(grad, grad_out, out_sems.at[1])
    store_grad.start()
    store_own = pltpu.make_async_copy(zgath.at[pl.ds(0, half)], half_of(wg_out, my_c), out_sems.at[2])
    store_own.start()
    wait_for(cgath, sems.at[17])
    store_other = pltpu.make_async_copy(cgath, half_of(wg_out, other), out_sems.at[3])
    store_other.start()

    drain(rows_a, up_a, down_a, chain_a, sems_a)
    drain(rows_b, up_b, down_b, chain_b, sems_b)
    wait_for(meta_out.at[pl.ds(0, 6)], sems.at[4])
    wait_for(meta_out.at[pl.ds(0, 2)], sems.at[18])
    wait_for(crecv, sems.at[6])
    wait_for(zsend.at[pl.ds(0, (en - 1) * piece)], sems.at[8])
    wait_for(ygot.at[pl.ds(0, YN - 1)], sems.at[12])
    wait_for(zgath.at[pl.ds(0, (en - 1) * piece)], sems.at[14])
    wait_for(cgath, sems.at[16])
    store_act.wait()
    store_grad.wait()
    store_own.wait()
    store_other.wait()


def finish(scale, act_in, grad_in, wg_in, act_out, grad_out, wg_out):
    act_out[...] = act_in[...]
    grad_out[...] = grad_in[...]
    wg_out[...] = wg_in[...].astype(F32) * scale


def on_device(zn, gn, features, occupancy, weights, cotangent, send_count, send_face, recv_face):
    vmem = pl.BlockSpec(memory_space=pltpu.VMEM)
    anywhere = pl.BlockSpec(memory_space=pltpu.HBM)
    xc_n = XN * CN
    half = TAPS * CH // CN
    en = zn * XN
    piece = -(-half // (16 * en)) * 16
    scale = float(zn * gn * ROWS) ** (-0.5)
    shells = [pltpu.VMEM((FACES, 64, CH), BF) for _ in range(3)]
    activated, grad, weight_grad = pl.pallas_call(
        functools.partial(kernel, zn, gn),
        out_shape=(
            jax.ShapeDtypeStruct((ROWS, CH), BF),
            jax.ShapeDtypeStruct((ROWS, CH), BF),
            jax.ShapeDtypeStruct((TAPS * CH, CH), BF),
        ),
        in_specs=[anywhere] * 7,
        out_specs=(anywhere, anywhere, anywhere),
        scratch_shapes=[
            pltpu.VMEM((ROWS, CH), BF),
            pltpu.VMEM((NB, VOX), jnp.int32),
            pltpu.VMEM((TAPS * CH, CH), BF),
            pltpu.VMEM((ROWS, CH), BF),
            pltpu.SMEM((gn,), jnp.int32),
            pltpu.SMEM((gn,), jnp.int32),
            pltpu.SMEM((gn,), jnp.int32),
            pltpu.VMEM((ROWS, CH), F32),
            pltpu.VMEM((ROWS, CH), F32),
            pltpu.VMEM((FACES, 64, CH), F32),
            pltpu.VMEM((VOX, CH), F32),
            pltpu.VMEM((ROWS, TAPS * CH), BF),
            pltpu.VMEM((TAPS * CH, CH), BF),
            pltpu.VMEM((CH, ROWS), BF),
            pltpu.VMEM((gn + 1, 64, CH), F32),
            pltpu.SMEM((gn,), jnp.int32),
            pltpu.SMEM((gn,), jnp.int32),
            pltpu.SMEM((gn,), jnp.int32),
            pltpu.SMEM((YN, 2 * xc_n), jnp.int32),
            pltpu.SMEM((YN, 2 * xc_n), jnp.int32),
            pltpu.SMEM((YN, 2 * xc_n), jnp.int32),
            pltpu.VMEM((FACES, 64, CH), BF),
            pltpu.VMEM((FACES, 64, CH), BF),
            pltpu.VMEM((xc_n, 8, 64, CH), BF),
            pltpu.VMEM((xc_n, 8, 64, CH), BF),
            pltpu.VMEM((xc_n, 8, 64, CH), BF),
            pltpu.VMEM((xc_n, 8, 64, CH), BF),
            shells, shells, shells, shells,
            pltpu.VMEM((TAPS * CH, CH), F32),
            pltpu.VMEM((half, CH), F32),
            pltpu.VMEM((en * piece, CH), BF),
            pltpu.VMEM((en, piece, CH), BF),
            pltpu.VMEM((YN, piece, CH), F32),
            pltpu.VMEM((en * piece, CH), BF),
            pltpu.VMEM((half, CH), BF),
            pltpu.VMEM((ROWS, CH), BF),
            pltpu.VMEM((ROWS, CH), BF),
            pltpu.SemaphoreType.DMA((7,)),
            pltpu.SemaphoreType.DMA((4,)),
            pltpu.SemaphoreType.DMA((24,)),
            pltpu.SemaphoreType.DMA((24,)),
            pltpu.SemaphoreType.DMA((20,)),
        ],
        compiler_params=pltpu.CompilerParams(
            collective_id=0, has_side_effects=True, vmem_limit_bytes=62 * 1024 * 1024
        ),
        cost_estimate=pl.CostEstimate(
            flops=6 * ROWS * TAPS * CH * CH, bytes_accessed=2000000, transcendentals=ROWS * CH
        ),
    )(
        features.reshape(ROWS, CH),
        occupancy,
        weights.reshape(TAPS * CH, CH),
        cotangent.reshape(ROWS, CH),
        send_count.reshape(gn),
        send_face.reshape(gn),
        recv_face.reshape(gn),
    )
    activated, grad, weight_grad = pl.pallas_call(
        functools.partial(finish, scale),
        out_shape=(
            jax.ShapeDtypeStruct((ROWS, CH), BF),
            jax.ShapeDtypeStruct((ROWS, CH), BF),
            jax.ShapeDtypeStruct((TAPS * CH, CH), F32),
        ),
        in_specs=[vmem, vmem, vmem],
        out_specs=(vmem, vmem, vmem),
        compiler_params=pltpu.CompilerParams(vmem_limit_bytes=62 * 1024 * 1024),
    )(activated, grad, weight_grad)
    return (
        activated.reshape(NB, VOX, CH),
        grad.reshape(NB, VOX, CH),
        weight_grad.reshape(TAPS, CH, CH),
    )


def solution(mesh):
    zn, gn = mesh.shape["gx"], mesh.shape["gy"]
    split = P(("gx", "gy"), None, None)
    return jax.shard_map(
        functools.partial(on_device, zn, gn),
        mesh=mesh,
        in_specs=(split, P(("gx", "gy"), None), P(), split, P(("gx", "gy"), None), split, split),
        out_specs=(split, split, P()),
        check_vma=False,
    )
```

```python
import functools

import jax
import jax.numpy as jnp
from jax import lax
from jax.experimental import pallas as pl
from jax.experimental.pallas import tpu as pltpu
from jax.sharding import PartitionSpec as P

XN = 4
YN = 8
CN = 2
MESH = pl.DeviceIdType.MESH
CH = 128
NB = 2
FACES = NB * 6
VOX = 512
ROWS = NB * VOX
TAPS = 7
OPPOSITE = (0, 2, 1, 4, 3, 6, 5)
BF = jnp.bfloat16
F32 = jnp.float32


def product(a, b):
    return jnp.dot(a, b, preferred_element_type=F32)


def cut_faces(cube, faces):
    for b in range(NB):
        base = b * VOX
        body = cube[base : base + VOX, :].reshape(8, 8, 8, CH)
        faces[b * 6 + 0] = cube[base : base + 64, :].astype(BF)
        faces[b * 6 + 1] = cube[base + 448 : base + 512, :].astype(BF)
        faces[b * 6 + 2] = body[:, 0].reshape(64, CH).astype(BF)
        faces[b * 6 + 3] = body[:, 7].reshape(64, CH).astype(BF)
        faces[b * 6 + 4] = cube[pl.ds(base, 64, stride=8), :].astype(BF)
        faces[b * 6 + 5] = cube[pl.ds(base + 7, 64, stride=8), :].astype(BF)


def build_views(cube, ghost, shifted, views):
    for b in range(NB):
        base = b * VOX
        rows = slice(base, base + VOX)
        g = b * 6
        body = cube[rows, :]
        solid = body.reshape(8, 8, 8, CH)
        views[rows, 0:128] = body.astype(BF)
        views[base : base + 64, 128:256] = ghost[g + 0].astype(BF)
        views[base + 64 : base + 512, 128:256] = cube[base : base + 448, :].astype(BF)
        views[base : base + 448, 256:384] = cube[base + 64 : base + 512, :].astype(BF)
        views[base + 448 : base + 512, 256:384] = ghost[g + 1].astype(BF)
        low = ghost[g + 2].reshape(8, 1, 8, CH)
        high = ghost[g + 3].reshape(8, 1, 8, CH)
        views[rows, 384:512] = jnp.concatenate([low, solid[:, :7]], axis=1).reshape(VOX, CH).astype(BF)
        views[rows, 512:640] = jnp.concatenate([solid[:, 1:], high], axis=1).reshape(VOX, CH).astype(BF)
        shifted[1:VOX, :] = cube[base : base + VOX - 1, :]
        shifted[pl.ds(0, 64, stride=8), :] = ghost[g + 4]
        views[rows, 640:768] = shifted[...].astype(BF)
        shifted[0 : VOX - 1, :] = cube[base + 1 : base + VOX, :]
        shifted[pl.ds(7, 64, stride=8), :] = ghost[g + 5]
        views[rows, 768:896] = shifted[...].astype(BF)


ROW_OF = (0, -1, 1, -2, 2, -3, 3, 4)
PIECES = 3


def kernel(
    zn, gn,
    feat_in, occ_in, wcat_in, cot_in, count_in, sface_in, rface_in,
    act_out, grad_out, wg_out,
    feat, occ, wcat, cot, count, sface, rface,
    mask, cube, ghost, shifted, views, wback, delta_t, run, prev, slot_face, slot_row, meta_out, meta_in, meta_far,
    faces_a, faces_b, rows_a, rows_b, got_a, got_b, up_a, down_a, up_b, down_b,
    csend, crecv, zsend, zrecv, ygot, zgath, cgath, act, grad, inner,
    load_sems, out_sems, chain_a, chain_b, sems_a, sems_b, sems,
):
    z = lax.axis_index("gx")
    me = lax.axis_index("gy")
    xc_n = XN * CN
    my_x = me // (YN * CN)
    my_y = lax.rem(me // CN, YN)
    my_c = lax.rem(me, CN)
    my_xc = my_x * CN + my_c
    half = TAPS * CH // CN
    en = zn * XN
    me_e = z * XN + my_x
    piece = zrecv.shape[1]

    def wrap_y(offset):
        return lax.rem(my_y + offset + YN, YN)

    def at(xc, y):
        return (xc // CN * YN + y) * CN + lax.rem(xc, CN)

    def xc_peer(k):
        return lax.rem(my_xc + k, xc_n)

    def each_zx(body):
        for dz in sorted(range(zn), key=lambda d: -min(d, zn - d)):
            first = lax.rem(z + dz, zn) * XN
            if dz:
                repeat(0, XN, lambda x: body(first + x))
            else:
                repeat(1, XN, lambda k: body(first + lax.rem(my_x + k, XN)))

    def zx_device(e):
        return (e // XN, at(lax.rem(e, XN) * CN + my_c, my_y))

    def repeat(low, high, body):
        def step(i, _):
            body(i)
            return 0

        lax.fori_loop(low, high, step, 0)

    def send(src, dst, send_sem, recv_sem, to):
        copy = pltpu.make_async_remote_copy(
            src_ref=src, dst_ref=dst, send_sem=send_sem, recv_sem=recv_sem, device_id=to, device_id_type=MESH
        )
        copy.start()

    def wait_for(ref, sem):
        pltpu.make_async_copy(ref, ref, sem).wait()

    loads = [
        pltpu.make_async_copy(src, dst, load_sems.at[i])
        for i, (src, dst) in enumerate(
            [(occ_in, occ), (feat_in, feat), (sface_in, sface), (rface_in, rface), (count_in, count), (wcat_in, wcat),
             (cot_in, cot)]
        )
    ]
    for load in loads[:2]:
        load.start()

    barrier = pltpu.get_barrier_semaphore()

    def greet(to):
        pl.semaphore_signal(barrier, inc=1, device_id=to, device_id_type=MESH)

    each_zx(lambda e: greet(zx_device(e)))
    repeat(1, YN, lambda k: greet((z, at(my_xc, wrap_y(k)))))
    repeat(1, xc_n, lambda k: greet((z, at(xc_peer(k), my_y))))
    repeat(1, xc_n, lambda k: greet((z, at(xc_peer(k), wrap_y(1)))))
    repeat(1, xc_n, lambda k: greet((z, at(xc_peer(k), wrap_y(-1)))))

    for load in loads[2:]:
        load.start()

    diagonal = lax.broadcasted_iota(jnp.int32, (CH, CH), 0) == lax.broadcasted_iota(jnp.int32, (CH, CH), 1)
    ones = jnp.ones((CH, CH), BF)
    loads[0].wait()
    loads[1].wait()
    for b in range(NB):
        for i in range(VOX // CH):
            row = (occ[b : b + 1, i * CH : (i + 1) * CH] > 0).astype(F32)
            spread = jnp.where(diagonal, jnp.broadcast_to(row, (CH, CH)), 0.0).astype(BF)
            place = b * VOX + i * CH
            flags = product(spread, ones)
            mask[place : place + CH, :] = flags
            cube[place : place + CH, :] = jnp.where(flags > 0, feat[place : place + CH, :].astype(F32), 0.0)
    cut_faces(cube, faces_a)
    def start_chain(faces, up, down, chain):
        for p in range(PIECES):
            part = pl.ds(p * (FACES // PIECES), FACES // PIECES)
            send(faces.at[part], up[0].at[part], chain.at[0], chain.at[6 + p], (z, at(my_xc, wrap_y(1))))
            send(faces.at[part], down[0].at[part], chain.at[3], chain.at[6 + 3 * PIECES + p], (z, at(my_xc, wrap_y(-1))))

    def start_row(faces, column, rows, got, up, down, chain, row_sems):
        def ship(k):
            xc = xc_peer(k)
            rows[xc, 0] = faces[meta_out[my_y, column + xc]]
            send(rows.at[xc, 0], got.at[my_xc, 0], row_sems.at[0], row_sems.at[1], (z, at(xc, my_y)))

        repeat(1, xc_n, ship)
        got[my_xc, 0] = faces[meta_out[my_y, column + my_xc]]

    def step_exchange(d, column, rows, got, up, down, chain, row_sems):
        for p in range(PIECES):
            part = pl.ds(p * (FACES // PIECES), FACES // PIECES)
            wait_for(up[d - 1].at[part], chain.at[6 + (d - 1) * PIECES + p])
            if d < 3:
                send(up[d - 1].at[part], up[d].at[part], chain.at[d], chain.at[6 + d * PIECES + p],
                     (z, at(my_xc, wrap_y(1))))
            wait_for(down[d - 1].at[part], chain.at[6 + (d + 2) * PIECES + p])
            if d < 3:
                send(down[d - 1].at[part], down[d].at[part], chain.at[3 + d], chain.at[6 + (d + 3) * PIECES + p],
                     (z, at(my_xc, wrap_y(-1))))
        if column == 0 and d == 1:
            wait_for(meta_in.at[pl.ds(0, 6)], sems.at[5])
            wait_for(meta_far.at[pl.ds(0, 2)], sems.at[19])
        low, high = wrap_y(-d), wrap_y(d)

        pair = pl.ds(2 * d - 1, 2)
        landed = row_sems.at[1 + d]

        def ship(k):
            xc = xc_peer(k)
            rows[xc, 2 * d - 1] = up[d - 1][meta_in[low, column + xc]]
            rows[xc, 2 * d] = down[d - 1][meta_in[high, column + xc]]
            send(rows.at[xc, pair], got.at[my_xc, pair], row_sems.at[0], landed, (z, at(xc, my_y)))

        def ship_up(xc):
            rows[xc, 7] = up[2][meta_far[low, column + xc]]
            send(rows.at[xc, 7], got.at[my_xc, 7], row_sems.at[0], landed, (z, at(xc, wrap_y(1))))

        def ship_down(xc):
            rows[xc, 7] = down[2][meta_far[high, column + xc]]
            send(rows.at[xc, 7], got.at[my_xc, 7], row_sems.at[0], landed, (z, at(xc, wrap_y(-1))))

        if d == 3:
            repeat(0, xc_n // 2, ship_up)
            repeat(xc_n // 2, xc_n, ship_down)
        repeat(1, xc_n, ship)
        got[my_xc, 2 * d - 1] = up[d - 1][meta_in[low, column + my_xc]]
        got[my_xc, 2 * d] = down[d - 1][meta_in[high, column + my_xc]]

    remote_faces = (xc_n - 1) * 7 + xc_n

    def flat(ref):
        return ref.reshape(xc_n * 8, 64, CH).at[pl.ds(0, remote_faces)]

    def wait_group(g, got, row_sems):
        many = (xc_n - 1) * (2 if g else 1) + (xc_n if g == 3 else 0)
        wait_for(got.reshape(xc_n * 8, 64, CH).at[pl.ds(0, many)], row_sems.at[1 + g])

    def drain(rows, up, down, chain, row_sems):
        for d in range(3):
            wait_for(up[d], chain.at[d])
            wait_for(down[d], chain.at[3 + d])
        wait_for(flat(rows), row_sems.at[0])

    pl.semaphore_wait(barrier, (YN - 1) + 3 * (xc_n - 1) + (en - 1))
    first = (rows_a, got_a, up_a, down_a, chain_a, sems_a)
    second = (rows_b, got_b, up_b, down_b, chain_b, sems_b)
    start_chain(faces_a, up_a, down_a, chain_a)
    loads[2].wait()
    loads[3].wait()
    loads[4].wait()

    def fill_meta(y):
        for xc in range(xc_n):
            meta_out[y, xc] = sface[at(jnp.int32(xc), y)]
            meta_out[y, xc_n + xc] = jnp.maximum(rface[at(jnp.int32(xc), y)], 0)

    repeat(0, YN, fill_meta)

    for d in (1, -1, 2, -2, 3, -3):
        y = wrap_y(d)
        send(meta_out.at[y], meta_in.at[my_y], sems.at[4], sems.at[5], (z, at(my_xc, y)))
    for d in (3, -3):
        send(meta_out.at[wrap_y(4)], meta_far.at[my_y], sems.at[18], sems.at[19], (z, at(my_xc, wrap_y(d))))
    start_row(faces_a, 0, *first)

    step_exchange(1, 0, *first)
    step_exchange(2, 0, *first)

    step_exchange(3, 0, *first)

    def list_slots(xc):
        for s in range(8):
            p = at(xc, wrap_y(ROW_OF[s]))
            slot_row[s * xc_n + xc] = rface[p]
            slot_face[s * xc_n + xc] = jnp.where(count[p] > 0, sface[p], FACES)

    repeat(0, xc_n, list_slots)

    def find_source(j, found):
        row = slot_row[j]
        return tuple(jnp.where(row == f, j, found[f]) for f in range(FACES))

    source = lax.fori_loop(0, gn, find_source, tuple(jnp.int32(-1) for _ in range(FACES)))
    def chain_up(j, last):
        face = slot_face[j]
        before = jnp.int32(0)
        for f in range(FACES):
            before = jnp.where(face == f, last[f], before)
        prev[j] = before
        return tuple(jnp.where(face == f, j + 1, last[f]) for f in range(FACES))

    last = lax.fori_loop(0, gn, chain_up, tuple(jnp.int32(0) for _ in range(FACES)))
    loads[5].wait()
    loads[6].wait()
    for t in range(TAPS):
        o = OPPOSITE[t]
        wback[t * CH : (t + 1) * CH, :] = wcat[o * CH : (o + 1) * CH, :].astype(F32).T.astype(BF)

    for g in range(4):
        wait_group(g, got_a, sems_a)
    for f in range(FACES):
        j = jnp.maximum(source[f], 0)
        taken = got_a[lax.rem(j, xc_n), j // xc_n].astype(F32)
        ghost[f] = jnp.where(source[f] >= 0, taken, 0.0)

    build_views(cube, ghost, shifted, views)
    for b in range(2 * NB):
        rows = slice(b * VOX // 2, (b + 1) * VOX // 2)
        preact = product(views[rows, :], wcat[...])
        sigma = jax.nn.sigmoid(preact)
        flags = mask[rows, :]
        act[rows, :] = (flags * preact * sigma).astype(BF)
        delta = (cot[rows, :].astype(F32) * flags * sigma * (1.0 + preact * (1.0 - sigma))).astype(BF)
        cube[rows, :] = delta.astype(F32)
    cut_faces(cube, faces_b)
    start_chain(faces_b, up_b, down_b, chain_b)
    start_row(faces_b, xc_n, *second)
    store_act = pltpu.make_async_copy(act, act_out, out_sems.at[0])
    store_act.start()

    delta_t[...] = cube[...].T.astype(BF)
    for t in range(TAPS):
        csend[t * CH : (t + 1) * CH, :] = product(delta_t[...], views[:, t * CH : (t + 1) * CH]).T
    other = 1 - my_c
    twin = (z, at(my_x * CN + other, my_y))

    def half_of(ref, c):
        return ref.at[pl.ds(pl.multiple_of(c * half, 16), half)]

    send(half_of(csend, other), crecv, sems.at[6], sems.at[7], twin)
    wait_for(crecv, sems.at[7])
    total = half_of(csend, my_c)[...] + crecv[...]
    zsend[0:half, :] = total.astype(BF)
    if en * piece > half:
        zsend[half:, :] = jnp.zeros((en * piece - half, CH), BF)

    def piece_of(ref, e):
        return ref.at[pl.ds(pl.multiple_of(e * piece, 16), piece)]

    def scatter(e):
        send(piece_of(zsend, e), zrecv.at[me_e], sems.at[8], sems.at[9], zx_device(e))

    each_zx(scatter)
    zrecv[me_e] = piece_of(zsend, me_e)[...]
    step_exchange(1, xc_n, *second)

    ghost[...] = jnp.zeros(ghost.shape, F32)
    build_views(cube, ghost, shifted, views)
    for b in range(2 * NB):
        rows = slice(b * VOX // 2, (b + 1) * VOX // 2)
        inner[rows, :] = product(views[rows, :], wback[...])

    run[0] = jnp.zeros((64, CH), F32)

    def add_up(g):
        wait_group(g, got_b, sems_b)
        for s in ((0,), (1, 2), (3, 4), (5, 6, 7))[g]:
            def add_one(xc, s=s):
                run[s * xc_n + xc + 1] = run[prev[s * xc_n + xc]] + got_b[xc, s].astype(F32)

            repeat(0, xc_n, add_one)

    step_exchange(2, xc_n, *second)
    add_up(0)
    wait_for(zrecv.at[pl.ds(0, en - 1)], sems.at[9])
    ygot[my_y] = jnp.sum(zrecv[...].astype(F32), axis=0)
    repeat(1, YN, lambda k: send(
        ygot.at[my_y], ygot.at[my_y], sems.at[12], sems.at[13], (z, at(my_xc, wrap_y(k)))))
    step_exchange(3, xc_n, *second)
    add_up(1)
    wait_for(ygot.at[pl.ds(0, YN - 1)], sems.at[13])
    total = ygot[0]
    for k in range(1, YN):
        total = total + ygot[k]
    mine = piece_of(zgath, me_e)
    mine[...] = total.astype(BF)
    each_zx(lambda e: send(mine, mine, sems.at[14], sems.at[15], zx_device(e)))

    add_up(2)
    add_up(3)
    for side in range(6):
        faces = jnp.concatenate([run[last[b * 6 + side]] for b in range(NB)], axis=0).astype(BF)
        layers = product(faces, wback[(1 + side) * CH : (2 + side) * CH, :])
        for b in range(NB):
            base = b * VOX
            layer = layers[b * 64 : (b + 1) * 64, :]
            if side < 2:
                first_row = base + 448 * side
                inner[first_row : first_row + 64, :] += layer
            elif side < 4:
                for x in range(8):
                    first_row = base + x * 64 + 56 * (side - 2)
                    inner[first_row : first_row + 8, :] += layer[x * 8 : (x + 1) * 8, :]
            else:
                inner[pl.ds(base + 7 * (side - 4), 64, stride=8), :] += layer
    grad[...] = (mask[...] * inner[...]).astype(BF)
    store_grad = pltpu.make_async_copy(grad, grad_out, out_sems.at[1])
    store_grad.start()
    wait_for(zgath.at[pl.ds(0, (en - 1) * piece)], sems.at[15])
    send(zgath.at[pl.ds(0, half)], cgath, sems.at[16], sems.at[17], twin)
    store_own = pltpu.make_async_copy(zgath.at[pl.ds(0, half)], half_of(wg_out, my_c), out_sems.at[2])
    store_own.start()
    wait_for(cgath, sems.at[17])
    store_other = pltpu.make_async_copy(cgath, half_of(wg_out, other), out_sems.at[3])
    store_other.start()

    drain(rows_a, up_a, down_a, chain_a, sems_a)
    drain(rows_b, up_b, down_b, chain_b, sems_b)
    wait_for(meta_out.at[pl.ds(0, 6)], sems.at[4])
    wait_for(meta_out.at[pl.ds(0, 2)], sems.at[18])
    wait_for(crecv, sems.at[6])
    wait_for(zsend.at[pl.ds(0, (en - 1) * piece)], sems.at[8])
    wait_for(ygot.at[pl.ds(0, YN - 1)], sems.at[12])
    wait_for(zgath.at[pl.ds(0, (en - 1) * piece)], sems.at[14])
    wait_for(cgath, sems.at[16])
    store_act.wait()
    store_grad.wait()
    store_own.wait()
    store_other.wait()


def finish(scale, act_in, grad_in, wg_in, act_out, grad_out, wg_out):
    act_out[...] = act_in[...]
    grad_out[...] = grad_in[...]
    wg_out[...] = wg_in[...].astype(F32) * scale


def on_device(zn, gn, features, occupancy, weights, cotangent, send_count, send_face, recv_face):
    vmem = pl.BlockSpec(memory_space=pltpu.VMEM)
    anywhere = pl.BlockSpec(memory_space=pltpu.HBM)
    xc_n = XN * CN
    half = TAPS * CH // CN
    en = zn * XN
    piece = -(-half // (16 * en)) * 16
    scale = float(zn * gn * ROWS) ** (-0.5)
    shells = [pltpu.VMEM((FACES, 64, CH), BF) for _ in range(3)]
    activated, grad, weight_grad = pl.pallas_call(
        functools.partial(kernel, zn, gn),
        out_shape=(
            jax.ShapeDtypeStruct((ROWS, CH), BF),
            jax.ShapeDtypeStruct((ROWS, CH), BF),
            jax.ShapeDtypeStruct((TAPS * CH, CH), BF),
        ),
        in_specs=[anywhere] * 7,
        out_specs=(anywhere, anywhere, anywhere),
        scratch_shapes=[
            pltpu.VMEM((ROWS, CH), BF),
            pltpu.VMEM((NB, VOX), jnp.int32),
            pltpu.VMEM((TAPS * CH, CH), BF),
            pltpu.VMEM((ROWS, CH), BF),
            pltpu.SMEM((gn,), jnp.int32),
            pltpu.SMEM((gn,), jnp.int32),
            pltpu.SMEM((gn,), jnp.int32),
            pltpu.VMEM((ROWS, CH), F32),
            pltpu.VMEM((ROWS, CH), F32),
            pltpu.VMEM((FACES, 64, CH), F32),
            pltpu.VMEM((VOX, CH), F32),
            pltpu.VMEM((ROWS, TAPS * CH), BF),
            pltpu.VMEM((TAPS * CH, CH), BF),
            pltpu.VMEM((CH, ROWS), BF),
            pltpu.VMEM((gn + 1, 64, CH), F32),
            pltpu.SMEM((gn,), jnp.int32),
            pltpu.SMEM((gn,), jnp.int32),
            pltpu.SMEM((gn,), jnp.int32),
            pltpu.SMEM((YN, 2 * xc_n), jnp.int32),
            pltpu.SMEM((YN, 2 * xc_n), jnp.int32),
            pltpu.SMEM((YN, 2 * xc_n), jnp.int32),
            pltpu.VMEM((FACES, 64, CH), BF),
            pltpu.VMEM((FACES, 64, CH), BF),
            pltpu.VMEM((xc_n, 8, 64, CH), BF),
            pltpu.VMEM((xc_n, 8, 64, CH), BF),
            pltpu.VMEM((xc_n, 8, 64, CH), BF),
            pltpu.VMEM((xc_n, 8, 64, CH), BF),
            shells, shells, shells, shells,
            pltpu.VMEM((TAPS * CH, CH), F32),
            pltpu.VMEM((half, CH), F32),
            pltpu.VMEM((en * piece, CH), BF),
            pltpu.VMEM((en, piece, CH), BF),
            pltpu.VMEM((YN, piece, CH), F32),
            pltpu.VMEM((en * piece, CH), BF),
            pltpu.VMEM((half, CH), BF),
            pltpu.VMEM((ROWS, CH), BF),
            pltpu.VMEM((ROWS, CH), BF),
            pltpu.VMEM((ROWS, CH), F32),
            pltpu.SemaphoreType.DMA((7,)),
            pltpu.SemaphoreType.DMA((4,)),
            pltpu.SemaphoreType.DMA((6 + 6 * PIECES,)),
            pltpu.SemaphoreType.DMA((6 + 6 * PIECES,)),
            pltpu.SemaphoreType.DMA((5,)),
            pltpu.SemaphoreType.DMA((5,)),
            pltpu.SemaphoreType.DMA((20,)),
        ],
        compiler_params=pltpu.CompilerParams(
            collective_id=0, has_side_effects=True, vmem_limit_bytes=62 * 1024 * 1024
        ),
        cost_estimate=pl.CostEstimate(
            flops=6 * ROWS * TAPS * CH * CH, bytes_accessed=2000000, transcendentals=ROWS * CH
        ),
    )(
        features.reshape(ROWS, CH),
        occupancy,
        weights.reshape(TAPS * CH, CH),
        cotangent.reshape(ROWS, CH),
        send_count.reshape(gn),
        send_face.reshape(gn),
        recv_face.reshape(gn),
    )
    activated, grad, weight_grad = pl.pallas_call(
        functools.partial(finish, scale),
        out_shape=(
            jax.ShapeDtypeStruct((ROWS, CH), BF),
            jax.ShapeDtypeStruct((ROWS, CH), BF),
            jax.ShapeDtypeStruct((TAPS * CH, CH), F32),
        ),
        grid=(2,),
        in_specs=[pl.BlockSpec((n, CH), lambda i: (i, 0)) for n in (512, 512, 448)],
        out_specs=tuple(pl.BlockSpec((n, CH), lambda i: (i, 0)) for n in (512, 512, 448)),
        compiler_params=pltpu.CompilerParams(vmem_limit_bytes=62 * 1024 * 1024),
    )(activated, grad, weight_grad)
    return (
        activated.reshape(NB, VOX, CH),
        grad.reshape(NB, VOX, CH),
        weight_grad.reshape(TAPS, CH, CH),
    )


def solution(mesh):
    zn, gn = mesh.shape["gx"], mesh.shape["gy"]
    split = P(("gx", "gy"), None, None)
    return jax.shard_map(
        functools.partial(on_device, zn, gn),
        mesh=mesh,
        in_specs=(split, P(("gx", "gy"), None), P(), split, P(("gx", "gy"), None), split, split),
        out_specs=(split, split, P()),
        check_vma=False,
    )
```
